32 devices in a mesh: seq: 8 (over z, y), exp: 4 (over x, core).
Axes of the slice: x: 2, y: 2, z: 4, core: 2. Of those that a mesh axis runs over, the one named last changes fastest.
Arguments:
- query_in: bfloat16 [4096, 2048], P('seq', 'exp'), may hold values from -0.52734375 to 0.52734375
- key_in: bfloat16 [4096, 2048], P('seq', 'exp'), may hold values from -0.52734375 to 0.52734375
- value_in: bfloat16 [4096, 2048], P('seq', 'exp'), may hold values from -0.52734375 to 0.52734375
- out_grad: bfloat16 [4096, 2048], P('seq', 'exp'), may hold values from -1.0546875 to 1.0546875
- inputs: bfloat16 [4096, 1024], P('seq'), may hold values from -0.13183594 to 0.13183594
- expert_ids: int32 [4096, 2], P('seq'), may hold values from 0 to 3, all different within a row; in each aligned block of 512 rows (0 to 511, 512 to 1023, ...) at most 384 rows name the same one
- route_gates: float32 [4096, 2], P('seq'), may hold values from 0.2 to 1
- expert_weight: bfloat16 [4, 1024, 4096], P('exp'), may hold values from -0.09375 to 0.09375
Outputs:
- gradient_of_queries: bfloat16 [4096, 2048], P('seq', 'exp')
- gradient_of_keys: bfloat16 [4096, 2048], P('seq', 'exp')
- value_grad: bfloat16 [4096, 2048], P('seq', 'exp')
- input_grad: bfloat16 [4096, 1024], P('seq', 'exp')
- weight_grad: float32 [4, 1024, 4096], P('exp', 'seq')
The draws below stay inside these ranges and needn't reach their ends.
Inputs may be any that keep to these rules, and one draw needn't show every extreme that they name: `expert_ids`: each token names two different experts. Among the 512 tokens of one index of seq no expert is named more than 384 times, a bound that some block reaches in some of them.
All inputs are finite; a program needn't handle non-finite values.
Results may differ from the reference program's by a relative error of at most 0.013.
Values may be sent and summed in bfloat16 or wider, within the bound.
No kernel may reach another device: no remote copies, remote signals or barrier semaphores. Data moves between devices by JAX's collectives and lax.ppermute only.
A program may use at most 128 MiB of HBM per device.

```python
import math
import jax
import jax.numpy as jnp
import numpy as np
from jax import lax

HEADS = 16
DH = 128
DIN = 1024
TOK_DEV = 512
TOKENS = 4096
EXPERTS = 4
CAP = 384
N_SEQ = 8


def with_spikes(values, key, source, target, blocks, factor):
    owner, partner = [(jnp.arange(values.shape[dim]) // (values.shape[dim] // blocks)).reshape([-1 if axis == dim else 1 for axis in range(values.ndim)]) for dim in (source, target)]
    chosen = jax.random.permutation(key, blocks)[partner]
    strong = (owner == chosen) | (owner == (partner + blocks // 2) % blocks)
    return jnp.where(strong, factor * values, values)


def levels(rng, dims, shards, smallest, top_value):
    loudness = 1.0
    for dim, shards_of in shards:
        draws = jax.random.uniform(jax.random.fold_in(jax.random.fold_in(rng, 6), dim), (shards_of,), jnp.float32, smallest / len(shards), top_value / len(shards))
        loudness = loudness * jnp.repeat(jnp.exp(draws), dims[dim] // shards_of).reshape((-1,) + (1,) * (len(dims) - 1 - dim))
    return loudness


def assign_block(stream_key, own, number, rows, count, top, reach, slope):
    ranking = jax.random.permutation(stream_key, count)
    crowded, ordinary = shares(count, rows * top, reach, slope, True), shares(count, rows * top, reach, slope, False)
    places = jnp.arange(count)

    def named(sizes, turn):
        used = int((sizes > 0).sum())
        fixed = max(1, used // 4)
        shifted = fixed + (places - fixed + turn * (used - fixed)) % max(1, count - fixed)
        return jnp.zeros((count,), jnp.int32).at[ranking[jnp.where(places < fixed, places, shifted)]].set(jnp.asarray(sizes, jnp.int32))

    sizes = jnp.where(number % 4 == 0, named(crowded, number // 4), named(ordinary, number - number // 4 - 1))
    mixed = jax.random.permutation(jax.random.fold_in(own, 3), count)
    giver, taker = mixed[0:count // 2 * 2:2], mixed[1:count // 2 * 2:2]
    room = jnp.minimum(sizes[giver] - 1, reach - sizes[taker]) // 2
    room = jnp.where((giver == ranking[0]) | (taker == ranking[0]) | (sizes[taker] == 0), 0, jnp.maximum(room, 0))
    shifted = jax.random.randint(jax.random.fold_in(own, 4), (count // 2,), 0, 1 << 20) % (room + 1)
    sizes = sizes.at[giver].add(-shifted).at[taker].add(shifted)
    labels = jnp.searchsorted(jnp.cumsum(sizes), jnp.arange(rows * top), side="right").astype(jnp.int32)
    table = labels.reshape(top, rows).T
    table = table[jax.random.permutation(jax.random.fold_in(own, 1), rows)]
    turn = jax.random.randint(jax.random.fold_in(own, 2), (rows, 1), 0, top)
    return jnp.take_along_axis(table, (jnp.arange(top)[None, :] + turn) % top, axis=1)


def shares(amount, total, limit, lean, full):
    portions = [(1 << 20) // math.isqrt(standing ** lean) + 1 for standing in range(1, amount + 1)]
    largest = limit if full else min(limit, max(-(-total // amount), total * portions[0] // sum(portions)))
    least = 1 if total - largest >= amount - 1 else 0
    counts, rest = [largest] + [least] * (amount - 1), total - largest - least * (amount - 1)
    while rest > 0:
        candidates = [i for i in range(1, amount) if counts[i] < largest] or [i for i in range(1, amount) if counts[i] < limit]
        pool, left = sum([portions[i] for i in candidates]), rest
        for i in candidates:
            extra = min(limit - counts[i], max(1, left * portions[i] // pool), rest)
            counts[i] = counts[i] + extra
            rest = rest - extra
    return np.array(counts)


def centred(rng, dims, deviation, bound, shards=(), kind=jnp.bfloat16):
    values = deviation * jax.random.normal(rng, dims, jnp.float32)
    if shards:
        values = values * levels(rng, dims, shards, -0.22, 0.18)
    return jnp.clip(values, -bound, bound).astype(kind)


def bell_draw_with(rng, extent, spread, most, pieces, heavy, kind=jnp.bfloat16):
    result = spread * jax.random.normal(rng, extent, jnp.float32)
    if pieces:
        result = result * levels(rng, extent, pieces, -0.22, 0.18)
    return jnp.clip(with_spikes(result, jax.random.fold_in(rng, 3), *heavy), -most, most).astype(kind)


def setup_inputs(seed: int = 0) -> dict:
    streams_of = jax.random.split(jax.random.key(seed), 9)
    query_in = centred(streams_of[0], (TOKENS, HEADS * DH), (DH ** -0.5), 0.52734375, ((0, 8), (1, 4)))
    key_in = centred(streams_of[1], (TOKENS, HEADS * DH), (DH ** -0.5), 0.52734375, ((0, 8), (1, 4)))
    value_in = centred(streams_of[2], (TOKENS, HEADS * DH), (DH ** -0.5), 0.52734375, ((0, 8), (1, 4)))
    out_grad = centred(streams_of[3], (TOKENS, HEADS * DH), ((DH / TOKENS) ** 0.5), 1.0546875, ((0, 8), (1, 4)))
    inputs = bell_draw_with(streams_of[4], (TOKENS, DIN), ((2 / TOKENS) ** 0.5), 0.13183594, ((0, 8),), (0, 1, 8, 2.0))
    expert_ids_keys = jax.random.split(jax.random.fold_in(streams_of[5], 1), TOKENS // TOK_DEV)
    expert_ids_turns = jax.random.permutation(jax.random.fold_in(streams_of[5], 3), TOKENS // TOK_DEV)
    expert_ids = jax.vmap(lambda own, number: assign_block(jax.random.fold_in(streams_of[5], 2), own, number, TOK_DEV, EXPERTS, 2, CAP, 2))(expert_ids_keys, expert_ids_turns).reshape((TOKENS, 2))
    route_gates = jnp.clip(0.2 + 0.8 * jax.random.uniform(streams_of[6], (TOKENS, 2), jnp.float32) ** levels(streams_of[6], (TOKENS, 2), ((0, 8),), -0.2, 0.2), 0.2, 1.0)
    expert_weight = centred(streams_of[7], (EXPERTS, DIN, 2 * HEADS * DH), (2 * HEADS * DH) ** -0.5, 0.09375, ((0, 4),))
    return {"query_in": query_in, "key_in": key_in, "value_in": value_in, "out_grad": out_grad, "inputs": inputs, "expert_ids": expert_ids, "route_gates": route_gates, "expert_weight": expert_weight}


highest_accuracy = lax.Precision.HIGHEST


def block_grads(backward_query, backward_key, backward_value, backward_gradient, leading_sum, trailing_sum):
    length = backward_query.shape[0]
    places = jnp.arange(length, dtype=jnp.int32)
    lower_triangle = (places[:, None] >= places[None, :])[None]
    upper_triangle = (places[:, None] <= places[None, :])[None]
    forward_query = backward_query.astype(jnp.float32)
    forward_key = backward_key.astype(jnp.float32)
    forward_value = backward_value.astype(jnp.float32)
    forward_gradient = backward_gradient.astype(jnp.float32)
    first_scores = jnp.where(lower_triangle, jnp.einsum('qnc,onc->nqo', forward_gradient, forward_value), 0.0).astype(jnp.bfloat16)
    middle_scores = jnp.where(upper_triangle, jnp.einsum('qnc,onc->nqo', forward_key, forward_query), 0.0).astype(jnp.bfloat16)
    third_scores = jnp.where(upper_triangle, jnp.einsum('qnc,onc->nqo', forward_value, forward_gradient), 0.0).astype(jnp.bfloat16)
    gradient_of_queries = jnp.einsum('wgq,qwn->gwn', first_scores.astype(jnp.float32), forward_key) + jnp.einsum('iok,osk->ios', forward_gradient, leading_sum, precision=highest_accuracy)
    gradient_of_keys = jnp.einsum('wgq,qwn->gwn', third_scores.astype(jnp.float32), forward_query) + jnp.einsum('iok,osk->ios', forward_value, trailing_sum, precision=highest_accuracy)
    value_grad = jnp.einsum('hlm,mhe->lhe', middle_scores.astype(jnp.float32), forward_gradient) + jnp.einsum('lhd,hde->lhe', forward_key, trailing_sum, precision=highest_accuracy)
    return gradient_of_queries.astype(jnp.bfloat16), gradient_of_keys.astype(jnp.bfloat16), value_grad.astype(jnp.bfloat16)


def reference(query_in, key_in, value_in, out_grad, inputs, expert_ids, route_gates, expert_weight):
    shape_four = (N_SEQ, TOK_DEV, HEADS, DH)
    backward_query = query_in.reshape(shape_four)
    backward_key = key_in.reshape(shape_four)
    backward_value = value_in.reshape(shape_four)
    backward_gradient = out_grad.reshape(shape_four)
    kv_sum = jnp.einsum('clhd,clhe->chde', backward_key.astype(jnp.float32), backward_value.astype(jnp.float32))
    qo_sum = jnp.einsum('clhd,clhe->chde', backward_query.astype(jnp.float32), backward_gradient.astype(jnp.float32))
    prefix_state = jnp.cumsum(kv_sum, axis=0) - kv_sum
    suffix_state = jnp.sum(qo_sum, axis=0)[None] - jnp.cumsum(qo_sum, axis=0)

    def one_block(packed):
        return block_grads(*packed)

    gradient_of_queries, gradient_of_keys, value_grad = lax.map(one_block, (backward_query, backward_key, backward_value, backward_gradient, prefix_state, suffix_state))
    gradient_of_queries = gradient_of_queries.reshape(TOKENS, HEADS * DH)
    gradient_of_keys = gradient_of_keys.reshape(TOKENS, HEADS * DH)
    value_grad = value_grad.reshape(TOKENS, HEADS * DH)
    kv_grad = jnp.concatenate([gradient_of_keys, value_grad], axis=1)
    input_acc = jnp.zeros((TOKENS, DIN), jnp.float32)
    weight_list = []
    for expert in range(EXPERTS):
        route_wt = jnp.sum(jnp.where(expert_ids == expert, route_gates, 0.0), axis=1)
        weighted = (route_wt[:, None] * inputs.astype(jnp.float32)).astype(jnp.bfloat16)
        weight_list.append(jnp.dot(weighted.T, kv_grad, preferred_element_type=jnp.float32))
        back_proj = lax.dot_general(kv_grad, expert_weight[expert], (((1,), (1,)), ((), ())), preferred_element_type=jnp.float32)
        input_acc = input_acc + route_wt[:, None] * back_proj
    return gradient_of_queries, gradient_of_keys, value_grad, input_acc.astype(jnp.bfloat16), jnp.stack(weight_list, axis=0)
```

```python
import functools

import jax
import jax.numpy as jnp
from jax import lax
from jax.experimental import pallas as pl
from jax.experimental.pallas import tpu as pltpu
from jax.sharding import PartitionSpec as P

DH = 128
PAD = 16
MIB = 1 << 20
BF16 = jnp.bfloat16
F32 = jnp.float32


def struct(shape, dtype):
    return jax.ShapeDtypeStruct(shape, dtype)


def call(kernel, out_shape, flops=0, moved=0, limit=16, **options):
    return pl.pallas_call(
        kernel,
        out_shape=out_shape,
        cost_estimate=pl.CostEstimate(flops=flops, bytes_accessed=moved, transcendentals=0),
        compiler_params=pltpu.CompilerParams(vmem_limit_bytes=limit * MIB),
        **options,
    )


def swap(array, axis, mask):
    count = lax.axis_size(axis)
    return lax.ppermute(array, axis, [(place, place ^ mask) for place in range(count)])


def shift(array, axis, step):
    count = lax.axis_size(axis)
    return lax.ppermute(array, axis, [(place, (place + step) % count) for place in range(count)])


def dot(a, b, left, right):
    return lax.dot_general(a, b, (((left,), (right,)), ((), ())), preferred_element_type=F32)


def head(ref, number):
    return ref[:, number * DH : (number + 1) * DH]


def own_states(first, second):
    rows, width = first.shape
    heads = width // DH

    def kernel(a_ref, b_ref, wide_ref, narrow_ref):
        for number in range(heads):
            state = dot(head(a_ref, number), head(b_ref, number), 0, 0)
            wide_ref[number] = state
            narrow_ref[number] = state.astype(BF16)

    return call(
        kernel,
        (struct((heads, DH, DH), F32), struct((heads, DH, DH), BF16)),
        flops=2 * rows * width * DH,
        moved=4 * rows * width,
    )(first, second)


def scan_states(total, sent, backward):
    count = lax.axis_size("seq")
    place = lax.axis_index("seq")
    state = jnp.zeros_like(total)
    mask = 1
    while mask < count:
        received = swap(sent, "seq", mask).astype(F32)
        lower = (place & mask) == 0
        state = state + jnp.where(lower == backward, received, 0.0)
        total = total + received
        sent = total.astype(BF16)
        mask *= 2
    return state


def triangle(size, lower):
    down = lax.broadcasted_iota(jnp.int32, (size, size), 0)
    across = lax.broadcasted_iota(jnp.int32, (size, size), 1)
    return down >= across if lower else down <= across


def intra_keys_values(query, key, value, grad):
    rows, width = query.shape
    heads = width // DH
    tile = rows // 2

    def kernel(q_ref, k_ref, v_ref, g_ref, out_ref):
        keep = triangle(tile, False)
        for down in range(2):
            here = pl.ds(down * tile, tile)
            rest = pl.ds(down * tile, rows - down * tile)
            for left, right, other, place in ((v_ref, g_ref, q_ref, 0), (k_ref, q_ref, g_ref, DH)):
                scores = dot(left[here, :], right[rest, :], 1, 1)
                first = jnp.where(keep, scores[:, :tile], 0.0).astype(BF16)
                if down == 0:
                    first = jnp.concatenate([first, scores[:, tile:].astype(BF16)], axis=1)
                out_ref[0, here, place : place + DH] = dot(first, other[rest, :], 1, 0)

    column = pl.BlockSpec((rows, DH), lambda number: (0, number))
    return call(
        kernel,
        struct((heads, rows, 2 * DH), F32),
        flops=6 * rows * rows * width,
        moved=16 * rows * width,
        grid=(heads,),
        in_specs=[column] * 4,
        out_specs=pl.BlockSpec((1, rows, 2 * DH), lambda number: (number, 0, 0)),
    )(query, key, value, grad)


def halves(state):
    high = state.astype(BF16)
    return high, (state - high.astype(F32)).astype(BF16)


def finish_keys_values(intra, key, value, suffix, number, within):
    rows = key.shape[0]

    def kernel(intra_ref, k_ref, v_ref, s_ref, out_ref):
        high, low = halves(s_ref[0])
        v, k = v_ref[...], k_ref[...]
        by_key = dot(v, high, 1, 1) + dot(v, low, 1, 1)
        by_value = dot(k, high, 1, 0) + dot(k, low, 1, 0)
        out_ref[:, :DH] = (intra_ref[0, :, :DH] + by_key).astype(BF16)
        out_ref[:, DH:] = (intra_ref[0, :, DH:] + by_value).astype(BF16)

    column = pl.BlockSpec((rows, DH), lambda step: (0, number))
    return call(
        kernel,
        struct((rows, 2 * DH), BF16),
        flops=8 * rows * DH * DH,
        moved=12 * rows * DH,
        grid=(1,),
        in_specs=[
            pl.BlockSpec((1, rows, 2 * DH), lambda step: (number, 0, 0)),
            column,
            column,
            pl.BlockSpec((1, DH, DH), lambda step: (within, 0, 0)),
        ],
        out_specs=pl.BlockSpec((rows, 2 * DH), lambda step: (0, 0)),
    )(intra, key, value, suffix)


def query_grads(key, value, grad, prefix):
    rows, width = key.shape
    heads = width // DH
    tile = rows // 2

    def kernel(k_ref, v_ref, g_ref, s_ref, out_ref):
        keep = triangle(tile, True)
        high, low = halves(s_ref[0])
        for down in range(2):
            here = pl.ds(down * tile, tile)
            upto = pl.ds(0, (down + 1) * tile)
            g = g_ref[here, :]
            scores = dot(g, v_ref[upto, :], 1, 1)
            last = jnp.where(keep, scores[:, down * tile :], 0.0).astype(BF16)
            if down:
                last = jnp.concatenate([scores[:, :tile].astype(BF16), last], axis=1)
            intra = dot(last, k_ref[upto, :], 1, 0)
            out_ref[here, :] = (intra + dot(g, high, 1, 1) + dot(g, low, 1, 1)).astype(BF16)

    column = pl.BlockSpec((rows, DH), lambda number: (0, number))
    return call(
        kernel,
        struct((rows, width), BF16),
        flops=3 * rows * rows * width,
        moved=8 * rows * width,
        grid=(heads,),
        in_specs=[column] * 3 + [pl.BlockSpec((1, DH, DH), lambda number: (number, 0, 0))],
        out_specs=column,
    )(key, value, grad, prefix)


def place_of():
    return jnp.stack([lax.axis_index("seq"), lax.axis_index("exp")]).astype(jnp.int32)


def prepare_inputs(inputs, ids, gates, place, size, experts, count):
    rows, wide = inputs.shape
    groups = count // size
    deep = wide // count

    def kernel(place_ref, x_ref, id_ref, gate_ref, *refs):
        outs, turned = refs[:size], refs[size]
        step = DH * 2
        for start in range(0, wide, step):
            turned[start : start + step, :] = x_ref[:, start : start + step].astype(F32).T.astype(BF16)
        which = lax.broadcasted_iota(jnp.int32, (experts, rows), 0)
        weight = jnp.zeros((experts, rows), F32)
        for slot in range(id_ref.shape[0]):
            weight += jnp.where(id_ref[slot : slot + 1, :] == which, gate_ref[slot : slot + 1, :], 0.0)
        parts = []
        for _ in range(3):
            part = weight.astype(BF16).astype(F32)
            parts.append(part)
            weight = weight - part
        tail = PAD - 3 * experts
        if tail:
            parts.append(jnp.zeros((tail, rows), F32))
        packed = jnp.concatenate(parts, axis=0).astype(BF16)
        me = place_ref[0]
        group, low = me // size, me % size
        for member in range(size):
            for hop in range(groups):
                block = lax.rem(group + hop, groups) * size + (low ^ member)
                source = pl.ds(pl.multiple_of(block * deep, deep), deep)
                outs[member][hop * deep : (hop + 1) * deep, :] = turned[source, :]
            outs[member][groups * deep :, :] = packed

    whole = pl.BlockSpec(memory_space=pltpu.VMEM)
    return call(
        kernel,
        [struct((groups * deep + PAD, rows), BF16)] * size,
        moved=4 * rows * wide,
        in_specs=[pl.BlockSpec(memory_space=pltpu.SMEM), whole, whole, whole],
        out_specs=[whole] * size,
        scratch_shapes=[pltpu.VMEM((wide, rows), BF16)],
    )(place, inputs, ids, gates)


def weigh_inputs(messages, place, experts):
    size = len(messages)
    deep, rows = messages[0].shape
    deep -= PAD

    def kernel(place_ref, *refs):
        out_ref = refs[size]
        expert = pl.program_id(0) ^ place_ref[1]
        for member in range(size):
            parts = refs[member][deep:, :].astype(F32)
            row = lax.broadcasted_iota(jnp.int32, parts.shape, 0)
            mine = (row < 3 * experts) & (lax.rem(row, experts) == expert)
            weight = jnp.sum(jnp.where(mine, parts, 0.0), axis=0, keepdims=True)
            out_ref[0, :, member * rows : (member + 1) * rows] = (
                refs[member][:deep, :].astype(F32) * weight
            ).astype(BF16)

    return call(
        kernel,
        struct((experts, deep, size * rows), BF16),
        flops=experts * deep * size * rows,
        moved=2 * (experts + 1) * deep * size * rows,
        grid_spec=pltpu.PrefetchScalarGridSpec(
            num_scalar_prefetch=1,
            grid=(experts,),
            in_specs=[pl.BlockSpec((deep + PAD, rows), lambda step, ref: (0, 0))] * size,
            out_specs=pl.BlockSpec((1, deep, size * rows), lambda step, ref: (step, 0, 0)),
        ),
    )(place, *messages)


def weight_product(weighted, blocks, groups):
    experts, deep, _ = weighted.shape
    rows, wide = blocks[0].shape
    size = len(blocks)
    part = deep // groups

    def kernel(w_ref, *refs):
        total = None
        for member in range(size):
            term = dot(w_ref[0, :, member * rows : (member + 1) * rows], refs[member][...], 1, 0)
            total = term if total is None else total + term
        refs[size][0] = total[:part]
        for hop in range(1, groups):
            refs[size + hop][0] = total[hop * part : (hop + 1) * part].astype(BF16)

    piece = pl.BlockSpec((1, part, wide), lambda step: (step, 0, 0))
    results = call(
        kernel,
        [struct((experts, part, wide), F32 if hop == 0 else BF16) for hop in range(groups)],
        flops=2 * experts * deep * size * rows * wide,
        moved=2 * experts * deep * size * rows + 2 * size * rows * wide + 4 * experts * deep * wide,
        grid=(experts,),
        in_specs=[pl.BlockSpec((1, deep, size * rows), lambda step: (step, 0, 0))]
        + [pl.BlockSpec((rows, wide), lambda step: (0, 0))] * size,
        out_specs=[piece] * groups,
    )(weighted, *blocks)
    return results[0], results[1:]


def add_partials(own, others):
    experts, part, wide = own.shape

    def kernel(own_ref, *refs):
        ins, outs = refs[: len(others)], refs[len(others) :]
        for expert in range(experts):
            total = own_ref[expert]
            for ref in ins:
                total = total + ref[expert].astype(F32)
            outs[expert][...] = total.astype(outs[expert].dtype)

    return call(
        kernel,
        [struct((part, wide), BF16 if expert else F32) for expert in range(experts)],
        moved=8 * experts * part * wide,
    )(own, *others)


def place_weight_grad(pieces, place, width):
    heads, experts = len(pieces), len(pieces[0])
    part = pieces[0][0].shape[0]

    def kernel(place_ref, *refs):
        out_ref = refs[heads * experts]
        for number in range(heads):
            for hop in range(experts):
                piece = refs[number * experts + hop]
                start = ((place_ref[1] ^ hop) * heads + number) * DH
                for side in range(2):
                    columns = pl.ds(pl.multiple_of(start + side * (width // 2), DH), DH)
                    out_ref[0, :, columns] = head(piece, side).astype(F32)

    whole = pl.BlockSpec(memory_space=pltpu.VMEM)
    return call(
        kernel,
        struct((1, part, width), F32),
        moved=6 * part * width,
        in_specs=[pl.BlockSpec(memory_space=pltpu.SMEM)] + [whole] * (heads * experts),
        out_specs=whole,
    )(place, *[piece for row in pieces for piece in row])


def place_keys_values(chunks):
    heads = len(chunks)
    rows = chunks[0].shape[0]

    def kernel(*refs):
        for number in range(heads):
            for side in range(2):
                refs[heads + side][:, number * DH : (number + 1) * DH] = head(refs[number], side)

    return call(kernel, [struct((rows, heads * DH), BF16)] * 2, moved=8 * rows * heads * DH)(*chunks)


def input_products(pieces, expert_weight, gate, place):
    experts, heads = len(pieces), len(pieces[0])
    rows = pieces[0][0].shape[0]
    _, wide, width = expert_weight.shape
    part = wide // experts

    def kernel(place_ref, w_ref, gate_ref, *refs):
        out_ref = refs[experts * heads]
        total = None
        for hop in range(experts):
            for number in range(heads):
                start = ((place_ref[1] ^ hop) * heads + number) * DH
                sides = [
                    w_ref[0, :, pl.ds(pl.multiple_of(start + side * (width // 2), DH), DH)]
                    for side in range(2)
                ]
                term = dot(refs[hop * heads + number][...], jnp.concatenate(sides, axis=1), 1, 1)
                total = term if total is None else total + term
        out_ref[0] = gate_ref[...] * total

    fixed = pl.BlockSpec((rows, 2 * DH), lambda step, ref: (0, 0))
    return call(
        kernel,
        struct((experts, rows, part), F32),
        flops=2 * rows * wide * width,
        moved=2 * wide * width + 2 * rows * width + 4 * rows * wide,
        limit=40,
        grid_spec=pltpu.PrefetchScalarGridSpec(
            num_scalar_prefetch=1,
            grid=(experts,),
            in_specs=[
                pl.BlockSpec((1, part, width), lambda step, ref: (0, step ^ ref[1], 0)),
                pl.BlockSpec((rows, 1), lambda step, ref: (0, 0)),
            ]
            + [fixed] * (experts * heads),
            out_specs=pl.BlockSpec((1, rows, part), lambda step, ref: (step, 0, 0)),
        ),
    )(place, expert_weight, gate, *[piece for row in pieces for piece in row])


def gather_exp(chunk, experts):
    held = [chunk]
    mask = experts // 2
    found = {0: chunk}
    while mask:
        for hop, array in list(found.items()):
            found[hop | mask] = swap(array, "exp", mask)
        mask //= 2
    return [found[hop] for hop in range(experts)]


def scatter_exp(parts):
    count = parts.shape[0]
    held = {hop: parts[hop] for hop in range(count)}
    mask = 1
    while mask < count:
        leaving = [hop for hop in sorted(held) if hop & mask]
        staying = [hop for hop in sorted(held) if not hop & mask]
        packed = jnp.stack([held[hop].astype(BF16) for hop in leaving])
        arrived = swap(packed, "exp", mask).astype(F32)
        held = {hop: held[hop] + arrived[at] for at, hop in enumerate(staying)}
        mask *= 2
    return held[0]


def per_device(query, key, value, grad, inputs, expert_ids, route_gates, expert_weight):
    rows, width = query.shape
    heads = width // DH
    experts = lax.axis_size("exp")
    count = lax.axis_size("seq")
    size = 4 if count % 4 == 0 else 1
    groups = count // size
    place = place_of()

    total, sent = own_states(query, grad)
    half = max(1, heads // 2)
    suffixes = [
        scan_states(total[at : at + half], sent[at : at + half], True) for at in range(0, heads, half)
    ]
    prefix = scan_states(*own_states(key, value), False)
    intra = intra_keys_values(query, key, value, grad)
    messages = prepare_inputs(
        inputs, expert_ids.T, route_gates.T, place, size, experts, count
    )
    messages = [messages[0]] + [swap(messages[mask], "seq", mask) for mask in range(1, size)]
    weighted = weigh_inputs(messages, place, experts)

    chunks = [
        finish_keys_values(intra, key, value, suffixes[number // half], number, number % half)
        for number in range(heads)
    ]
    pieces = []
    gathered = []
    for chunk in chunks:
        blocks = [chunk]
        if size == 4:
            across = swap(chunk, "seq", 2)
            blocks = [chunk, swap(chunk, "seq", 1), across, swap(across, "seq", 1)]
        gathered.append(gather_exp(chunk, experts))
        own, others = weight_product(weighted, blocks, groups)
        others = [shift(other, "seq", size * (hop + 1)) for hop, other in enumerate(others)]
        parts = add_partials(own, others)
        pieces.append([parts[0]] + [swap(parts[hop], "exp", hop) for hop in range(1, experts)])

    gradient_of_queries = query_grads(key, value, grad, prefix)
    gradient_of_keys, value_grad = place_keys_values(chunks)
    mine = expert_ids == lax.axis_index("exp")
    gate = jnp.sum(jnp.where(mine, route_gates, 0.0), axis=1, keepdims=True)
    returned = input_products(
        [[gathered[number][hop] for number in range(heads)] for hop in range(experts)],
        expert_weight,
        gate,
        place,
    )
    input_grad = scatter_exp(returned).astype(BF16)
    weight_grad = place_weight_grad(pieces, place, expert_weight.shape[2])
    return gradient_of_queries, gradient_of_keys, value_grad, input_grad, weight_grad


def solution(mesh):
    return jax.shard_map(
        per_device,
        mesh=mesh,
        in_specs=(
            P("seq", "exp"),
            P("seq", "exp"),
            P("seq", "exp"),
            P("seq", "exp"),
            P("seq", None),
            P("seq", None),
            P("seq", None),
            P("exp", None, None),
        ),
        out_specs=(
            P("seq", "exp"),
            P("seq", "exp"),
            P("seq", "exp"),
            P("seq", "exp"),
            P("exp", "seq", None),
        ),
        check_vma=False,
    )
```

```python
import functools

import jax
import jax.numpy as jnp
from jax import lax
from jax.experimental import pallas as pl
from jax.experimental.pallas import tpu as pltpu
from jax.sharding import PartitionSpec as P

DH = 128
PAD = 16
MIB = 1 << 20
BF16 = jnp.bfloat16
F32 = jnp.float32
VMEM = pl.BlockSpec(memory_space=pltpu.VMEM)
SMEM = pl.BlockSpec(memory_space=pltpu.SMEM)
HBM = pl.BlockSpec(memory_space=pltpu.HBM)


def struct(shape, dtype):
    return jax.ShapeDtypeStruct(shape, dtype)


TOKEN = struct((8, 128), F32)


def call(kernel, out_shape, operands, specs, wait=(), limit=16, cost=0, **options):
    known = len(operands)

    def body(*refs):
        kernel(*refs[:known], *refs[known + len(wait) :])

    grid = options.pop("grid", ())
    out_specs = options.pop("out_specs", VMEM)
    scratch = options.pop("scratch_shapes", ())
    prefetch = options.pop("prefetch", 0)
    if out_specs is VMEM and isinstance(out_shape, (list, tuple)):
        out_specs = [VMEM] * len(out_shape)
    return pl.pallas_call(
        body,
        out_shape=out_shape,
        grid_spec=pltpu.PrefetchScalarGridSpec(
            num_scalar_prefetch=prefetch,
            grid=grid,
            in_specs=list(specs) + [pl.BlockSpec(memory_space=pl.ANY)] * len(wait),
            out_specs=out_specs,
            scratch_shapes=scratch,
        ),
        cost_estimate=pl.CostEstimate(flops=cost, bytes_accessed=0, transcendentals=0),
        compiler_params=pltpu.CompilerParams(vmem_limit_bytes=limit * MIB),
        **options,
    )(*operands, *wait)


def swap(array, axis, mask):
    count = lax.axis_size(axis)
    return lax.ppermute(array, axis, [(place, place ^ mask) for place in range(count)])


def shift(array, axis, step):
    count = lax.axis_size(axis)
    return lax.ppermute(array, axis, [(place, (place + step) % count) for place in range(count)])


def dot(a, b, left, right):
    return lax.dot_general(a, b, (((left,), (right,)), ((), ())), preferred_element_type=F32)


def head(ref, number):
    return ref[:, number * DH : (number + 1) * DH]


def own_states(first, second, wait=()):
    rows, width = first.shape
    heads = width // DH

    def kernel(a_ref, b_ref, wide_ref, narrow_ref, a_kept, b_kept):
        for number in range(heads):
            state = dot(head(a_ref, number), head(b_ref, number), 0, 0)
            wide_ref[number] = state
            narrow_ref[number] = state.astype(BF16)
        a_kept[...] = a_ref[...]
        b_kept[...] = b_ref[...]

    shapes = [struct((heads, DH, DH), F32), struct((heads, DH, DH), BF16)] + [struct((rows, width), BF16)] * 2
    return call(kernel, shapes, (first, second), [VMEM] * 2, wait, cost=6 * rows * width * DH)


def after(array, *earlier):
    return lax.optimization_barrier((array, *earlier))[0]


def add_arrived(total, arrived, last, wait=()):
    def kernel(total_ref, arrived_ref, narrow_ref, *wide):
        added = total_ref[...] + arrived_ref[...].astype(F32)
        narrow_ref[...] = added.astype(BF16)
        for ref in wide:
            ref[...] = added

    shapes = [struct(total.shape, BF16)] + ([] if last else [struct(total.shape, F32)])
    sent, *total = call(kernel, shapes, (total, arrived), [VMEM] * 2, wait)
    return (total[0] if total else None), sent


def touch(wait):
    def kernel(out_ref):
        out_ref[...] = jnp.zeros_like(out_ref)

    return call(kernel, TOKEN, (), (), wait)


def stack(first, second, at, wait=()):
    def kernel(a_ref, b_ref, out_ref):
        for place, ref in enumerate((a_ref, b_ref)):
            out_ref[place] = ref[...] if at[place] is None else ref[at[place]]

    return call(kernel, struct((2, *first.shape[-2:]), first.dtype), (first, second), [VMEM] * 2, wait)


def gathered_state(place, refs, number, backward):
    state = None
    for step, ref in enumerate(refs):
        lower = ((place >> step) & 1) == 0
        term = jnp.where(lower == backward, ref[number].astype(F32), 0.0)
        state = term if state is None else state + term
    return state


def triangle(size, lower):
    down = lax.broadcasted_iota(jnp.int32, (size, size), 0)
    across = lax.broadcasted_iota(jnp.int32, (size, size), 1)
    return down >= across if lower else down <= across


def intra_keys_values(query, key, value, grad, first, many, wait=()):
    rows = query.shape[0]
    tile = rows // 2

    def kernel(q_ref, k_ref, v_ref, g_ref, out_ref):
        keep = triangle(tile, False)
        for number in range(many):
            q, k, v, g = (head(ref, first + number) for ref in (q_ref, k_ref, v_ref, g_ref))
            for down in range(2):
                here = slice(down * tile, (down + 1) * tile)
                rest = slice(down * tile, rows)
                for left, right, other, place in ((v, g, q, 0), (k, q, g, DH)):
                    scores = dot(left[here], right[rest], 1, 1)
                    kept = jnp.where(keep, scores[:, :tile], 0.0).astype(BF16)
                    if down == 0:
                        kept = jnp.concatenate([kept, scores[:, tile:].astype(BF16)], axis=1)
                    out_ref[number, here, place : place + DH] = dot(kept, other[rest], 1, 0)

    return call(
        kernel,
        struct((many, rows, 2 * DH), F32),
        (query, key, value, grad),
        [VMEM] * 4,
        wait,
        cost=24 * rows * rows * many * DH,
    )


def halves(state):
    high = state.astype(BF16)
    return high, (state - high.astype(F32)).astype(BF16)


def finish_keys_values(intra, key, value, arrived, place, sets, known=(), wait=()):
    where = [(array, at) for array in range(len(intra)) for at in range(intra[array].shape[0])]
    rows, wide = intra[0].shape[1:]
    needed = sorted({start + at for start, many in sets for at in range(many or 1)})

    def kernel(place_ref, k_ref, v_ref, *refs):
        states, refs = refs[: len(arrived)], refs[len(arrived) :]
        intra_refs, refs = refs[: len(intra)], refs[len(intra) :]
        known_refs, outs = refs[: len(known)], refs[len(known) :]
        for number in needed:
            if number < len(known):
                both = known_refs[number][...]
            else:
                high, low = halves(gathered_state(place_ref[0], states, number, True))
                v, k = head(v_ref, number), head(k_ref, number)
                by_key = dot(v, high, 1, 1) + dot(v, low, 1, 1)
                by_value = dot(k, high, 1, 0) + dot(k, low, 1, 0)
                array, at = where[number]
                both = intra_refs[array][at] + jnp.concatenate([by_key, by_value], axis=1)
                both = both.astype(BF16)
            for out, (start, many) in zip(outs, sets):
                if many is None and number == start:
                    out[...] = both
                elif many is not None and start <= number < start + many:
                    out[number - start] = both

    shapes = [struct((rows, wide) if many is None else (many, rows, wide), BF16) for _, many in sets]
    operands = (place, key, value, *arrived, *intra, *known)
    return call(kernel, shapes, operands, [SMEM] + [VMEM] * (len(operands) - 1), wait)


def query_grads(key, value, grad, arrived, place, wait=()):
    rows, width = key.shape
    heads = width // DH
    tile = rows // 2

    def kernel(place_ref, k_ref, v_ref, g_ref, *refs):
        out_ref, token_ref, done, sems = refs[len(arrived) :]
        token_ref[...] = jnp.zeros_like(token_ref)
        copies = []
        keep = triangle(tile, True)
        for number in range(heads):
            high, low = halves(gathered_state(place_ref[0], refs[: len(arrived)], number, False))
            k, v, grad_of = head(k_ref, number), head(v_ref, number), head(g_ref, number)
            for down in range(2):
                upto = (down + 1) * tile
                g = grad_of[down * tile : upto]
                scores = dot(g, v[:upto], 1, 1)
                last = jnp.where(keep, scores[:, down * tile :], 0.0).astype(BF16)
                if down:
                    last = jnp.concatenate([scores[:, :tile].astype(BF16), last], axis=1)
                intra = dot(last, k[:upto], 1, 0)
                whole_grad = intra + dot(g, high, 1, 1) + dot(g, low, 1, 1)
                done[number, down * tile : upto, :] = whole_grad.astype(BF16)
            columns = slice(number * DH, (number + 1) * DH)
            copies.append(pltpu.make_async_copy(done.at[number], out_ref.at[:, columns], sems.at[number]))
            copies[-1].start()
        for copy in copies:
            copy.wait()

    return call(
        kernel,
        [struct((rows, width), BF16), TOKEN],
        (place, key, value, grad, *arrived),
        [SMEM] + [VMEM] * (3 + len(arrived)),
        wait,
        cost=24 * rows * rows * width,
        out_specs=[HBM, VMEM],
        scratch_shapes=[pltpu.VMEM((heads, rows, DH), BF16), pltpu.SemaphoreType.DMA((heads,))],
    )


def place_of():
    return jnp.stack([lax.axis_index("seq"), lax.axis_index("exp")]).astype(jnp.int32)


def prepare_inputs(inputs, ids, gates, place, size, experts, count, wait=()):
    rows, wide = inputs.shape
    groups = count // size
    deep = wide // count
    half = rows // 2

    def kernel(place_ref, x_ref, id_ref, gate_ref, *refs):
        own_ref, one_ref, two_ref, column_ref, turned = refs
        outs = [own_ref, one_ref, two_ref.at[0], two_ref.at[1]]
        step = DH * 2
        for start in range(0, wide, step):
            turned[start : start + step, :] = x_ref[:, start : start + step].astype(F32).T.astype(BF16)
        which = lax.broadcasted_iota(jnp.int32, (experts, rows), 0)
        weight = jnp.zeros((experts, rows), F32)
        for slot in range(id_ref.shape[0]):
            weight += jnp.where(id_ref[slot : slot + 1, :] == which, gate_ref[slot : slot + 1, :], 0.0)
        mine = jnp.sum(jnp.where(which == place_ref[1], weight, 0.0), axis=0, keepdims=True)
        column_ref[...] = jnp.broadcast_to(mine, (8, rows)).T[:, :1]
        parts = []
        for _ in range(3):
            part = weight.astype(BF16).astype(F32)
            parts.append(part)
            weight = weight - part
        tail = PAD - 3 * experts
        if tail:
            parts.append(jnp.zeros((tail, rows), F32))
        packed = jnp.concatenate(parts, axis=0)
        me = place_ref[0]
        odd = place_ref[1] & 1
        group, low = me // size, me % size
        columns = pl.ds(pl.multiple_of(odd * half, half), half)
        side = jnp.where(odd == 1, packed[:, half:], packed[:, :half]).astype(BF16)
        for member in range(size):
            for hop in range(groups):
                block = lax.rem(group + hop, groups) * size + (low ^ member)
                source = pl.ds(pl.multiple_of(block * deep, deep), deep)
                part = turned[source, columns] if member else turned[source, :]
                outs[member][hop * deep : (hop + 1) * deep, :] = part
            outs[member][groups * deep :, :] = side if member else packed.astype(BF16)

    tall = groups * deep + PAD
    shapes = [struct((tall, rows), BF16), struct((tall, half), BF16), struct((2, tall, half), BF16)]
    return call(
        kernel,
        shapes + [struct((rows, 1), F32)],
        (place, inputs, ids, gates),
        [SMEM] + [VMEM] * 3,
        wait,
        scratch_shapes=[pltpu.VMEM((wide, rows), BF16)],
    )


def weigh_inputs(own, halves_of, place, experts, wait=()):
    deep, rows = own.shape
    deep -= PAD
    half = rows // 2
    size = 1 + len(halves_of)
    flat = [entry for pair in halves_of for entry in pair]

    def kernel(place_ref, own_ref, *refs):
        out_ref = refs[len(flat)]
        odd = place_ref[1] & 1
        for at in range(1 + len(flat)):
            ref = own_ref if at == 0 else refs[at - 1].at[flat[at - 1][1]]
            columns = ref[:deep, :].astype(F32)
            parts = ref[deep:, :].astype(F32)
            row = lax.broadcasted_iota(jnp.int32, parts.shape, 0)
            for step in range(experts):
                mine = (row < 3 * experts) & (lax.rem(row, experts) == (step ^ place_ref[1]))
                weight = jnp.sum(jnp.where(mine, parts, 0.0), axis=0, keepdims=True)
                scaled = (columns * weight).astype(BF16)
                if at == 0:
                    out_ref[step, :, :rows] = scaled
                else:
                    side = odd if at % 2 else 1 - odd
                    start = pl.multiple_of((at + 1) // 2 * rows + side * half, half)
                    out_ref[step, :, pl.ds(start, half)] = scaled

    return call(
        kernel,
        struct((experts, deep, size * rows), BF16),
        (place, own, *[array for array, _ in flat]),
        [SMEM] + [VMEM] * (1 + len(flat)),
        wait,
    )


def weight_product(weighted, blocks, groups, wait=()):
    experts, deep, _ = weighted.shape
    rows, wide = blocks[0][0].shape[-2:]
    size = len(blocks)
    part = deep // groups

    def kernel(w_ref, *refs):
        outs = refs[size:]
        for expert in range(experts):
            total = None
            for member in range(size):
                left = w_ref[expert, :, member * rows : (member + 1) * rows]
                at = blocks[member][1]
                right = refs[member][...] if at is None else refs[member][at]
                term = dot(left, right, 1, 0)
                total = term if total is None else total + term
            for hop in range(groups):
                piece = total[hop * part : (hop + 1) * part]
                outs[hop][expert] = piece.astype(outs[hop].dtype)

    results = call(
        kernel,
        [struct((experts, part, wide), BF16 if hop else F32) for hop in range(groups)],
        (weighted, *[array for array, _ in blocks]),
        [VMEM] * (1 + size),
        wait,
        cost=2 * experts * deep * size * rows * wide,
    )
    return results[0], results[1:]


def add_partials(owns, others, sets, wait=()):
    experts, part, wide = owns[0].shape
    chunks = len(owns)
    flat = [ref for chunk in range(chunks) for ref in (owns[chunk], *others[chunk])]
    each = len(flat) // chunks

    def kernel(*refs):
        outs = refs[len(flat) :]
        for chunk in range(chunks):
            for out, hops in zip(outs, sets):
                for at, hop in enumerate(hops):
                    total = refs[chunk * each][hop]
                    for ref in refs[chunk * each + 1 : (chunk + 1) * each]:
                        total = total + ref[hop].astype(F32)
                    out[at, chunk] = total.astype(out.dtype)

    return call(
        kernel,
        [struct((len(hops), chunks, part, wide), BF16 if hops[0] else F32) for hops in sets],
        flat,
        [VMEM] * len(flat),
        wait,
    )


def place_weight_grad(pieces, place, width):
    experts = len(pieces[0])
    counts = [row[0].shape[1] for row in pieces]
    heads = sum(counts)
    part = pieces[0][0].shape[2]
    flat = [piece for row in pieces for piece in row]
    slots = heads * experts * 2

    def kernel(place_ref, *refs):
        out_ref, ready, sems = refs[len(flat) :]
        copies = []
        number = 0
        for at, many in enumerate(counts):
            for within in range(many):
                for hop in range(experts):
                    start = ((place_ref[1] ^ hop) * heads + number) * DH
                    for side in range(2):
                        slot = (number * experts + hop) * 2 + side
                        piece = refs[at * experts + hop][0, within, :, side * DH : (side + 1) * DH]
                        ready[slot] = piece.astype(F32)
                        columns = pl.ds(pl.multiple_of(start + side * (width // 2), DH), DH)
                        copy = pltpu.make_async_copy(
                            ready.at[slot], out_ref.at[0, :, columns], sems.at[slot]
                        )
                        copy.start()
                        copies.append(copy)
                number += 1
        for copy in copies:
            copy.wait()

    return call(
        kernel,
        struct((1, part, width), F32),
        (place, *flat),
        [SMEM] + [VMEM] * len(flat),
        out_specs=HBM,
        scratch_shapes=[pltpu.VMEM((slots, part, DH), F32), pltpu.SemaphoreType.DMA((slots,))],
    )


def place_keys_values(chunks, wait=()):
    heads, rows, _ = chunks.shape

    def kernel(chunks_ref, *refs):
        token_ref, sems = refs[2:]
        token_ref[...] = jnp.zeros_like(token_ref)
        copies = []
        for number in range(heads):
            for side in range(2):
                source = chunks_ref.at[number, :, side * DH : (side + 1) * DH]
                target = refs[side].at[:, number * DH : (number + 1) * DH]
                copies.append(pltpu.make_async_copy(source, target, sems.at[number * 2 + side]))
        for copy in copies:
            copy.start()
        for copy in copies:
            copy.wait()

    return call(
        kernel,
        [struct((rows, heads * DH), BF16)] * 2 + [TOKEN],
        (chunks,),
        [VMEM],
        wait,
        out_specs=[HBM] * 2 + [VMEM],
        scratch_shapes=[pltpu.SemaphoreType.DMA((2 * heads,))],
    )


def input_products(pieces, expert_weight, gate, place, wait=()):
    experts = len(pieces)
    heads, rows, _ = pieces[0].shape
    _, wide, width = expert_weight.shape
    part = wide // experts
    even = experts // 2

    def kernel(place_ref, w_ref, gate_ref, *refs):
        keep_ref, send_ref = refs[experts:]
        for out in range(experts):
            taken = pl.ds(pl.multiple_of((place_ref[1] ^ out) * part, part), part)
            total = None
            for hop in range(experts):
                for number in range(heads):
                    start = ((place_ref[1] ^ hop) * heads + number) * DH
                    sides = [
                        w_ref[0, taken, pl.ds(pl.multiple_of(start + side * (width // 2), DH), DH)]
                        for side in range(2)
                    ]
                    term = dot(refs[hop][number], jnp.concatenate(sides, axis=1), 1, 1)
                    total = term if total is None else total + term
            total = gate_ref[...] * total
            if out % 2:
                send_ref[out // 2] = total.astype(BF16)
            else:
                keep_ref[out // 2] = total

    return call(
        kernel,
        [struct((even, rows, part), F32), struct((even, rows, part), BF16)],
        (place, expert_weight, gate, *pieces),
        [SMEM] + [VMEM] * (2 + experts),
        wait,
        cost=2 * rows * wide * width,
    )


def add_parts(keep, arrived, wait=()):
    count, rows, wide = keep.shape
    half = count // 2

    def kernel(keep_ref, arrived_ref, *outs):
        for at in range(count):
            total = keep_ref[at] + arrived_ref[at].astype(F32)
            if count == 1:
                outs[0][...] = total.astype(BF16)
            else:
                outs[at // half][at % half] = total.astype(outs[at // half].dtype)

    if count == 1:
        shapes = struct((rows, wide), BF16)
    else:
        shapes = [struct((half, rows, wide), F32), struct((half, rows, wide), BF16)]
    return call(kernel, shapes, (keep, arrived), [VMEM] * 2, wait)


def per_device(query, key, value, grad, inputs, expert_ids, route_gates, expert_weight):
    width = query.shape[1]
    heads = width // DH
    experts = lax.axis_size("exp")
    count = lax.axis_size("seq")
    size = 4
    groups = count // size
    many = heads // 2
    place = place_of()

    own_columns, one, two, gate = prepare_inputs(
        inputs, expert_ids.T, route_gates.T, place, size, experts, count
    )
    by_two = swap(two, "seq", 2)

    total, sent, query, grad = own_states(query, grad, [two])
    later = [swap(sent, "seq", 1)]
    other_total, other_sent, key, value = own_states(key, value, [sent])
    total, sent = add_arrived(total, later[0], False, [other_sent])
    later.append(swap(sent, "seq", 2))
    earlier = [swap(after(other_sent, sent), "seq", 1)]
    by_one = swap(stack(one, by_two, (None, 1), [sent]), "seq", 1)
    first_half = intra_keys_values(query, key, value, grad, 0, many, [sent])
    waits = [first_half]
    mask = 4
    while mask < count:
        total, sent = add_arrived(total, later[-1], 2 * mask >= count, waits)
        later.append(swap(sent, "seq", mask))
        other_total, other_sent = add_arrived(other_total, earlier[-1], False, [sent])
        earlier.append(swap(other_sent, "seq", mask // 2))
        waits = [other_sent]
        mask *= 2
    second_half = intra_keys_values(query, key, value, grad, many, heads - many, [sent])
    by_two_other, by_one_other = swap(by_two, "exp", 1), swap(by_one, "exp", 1)
    weighted = weigh_inputs(
        own_columns,
        [
            [(by_one, 0), (by_one_other, 0)],
            [(by_two, 0), (by_two_other, 0)],
            [(by_one, 1), (by_one_other, 1)],
        ],
        place,
        experts,
        [second_half],
    )
    other_total, other_sent = add_arrived(other_total, earlier[-1], True, [weighted])

    intra = [first_half, second_half]
    (lead,) = finish_keys_values(intra, key, value, later, place, [(0, None)], (), [other_sent])
    near = [(swap(lead, "seq", 1), None)]
    across = [(swap(lead, "seq", 2), None)]
    every, second, rest = finish_keys_values(
        intra, key, value, later, place, [(0, heads), (1, None), (2, heads - 2)], (lead,)
    )
    earlier.append(swap(after(other_sent, every), "seq", count // 2))
    across.append((swap(second, "seq", 2), None))
    rest = swap(rest, "seq", 2)
    across += [(rest, at) for at in range(heads - 2)]
    far = swap(every, "exp", 2)
    pieces = [every, swap(every, "exp", 1), far, swap(far, "exp", 1)]
    relayed = [(swap(after(across[0][0], near[0][0]), "seq", 1), None)]
    owns, others = [], []
    waits = []
    for number in range(heads):
        if number:
            stacked = stack(
                every, across[number][0], (number, across[number][1]), [relayed[number - 1][0]]
            )
            pair = swap(stacked, "seq", 1)
            near.append((pair, 0))
            relayed.append((pair, 1))
        if number == 1:
            gradient_of_keys, value_grad, token = place_keys_values(every, [stacked])
            waits = [token]
        elif number == 2:
            gradient_of_queries, token = query_grads(key, value, grad, earlier, place, [stacked])
            waits = [token]
        elif number == 3:
            keep, send = input_products(pieces, expert_weight, gate, place, [stacked])
            waits = [send]
        if number >= 2:
            waits.append(touch([*others[number - 2], owns[number - 1]]))
        own, other = weight_product(
            weighted, [(every, number), near[number], across[number], relayed[number]], groups, waits
        )
        owns.append(own)
        others.append([shift(array, "seq", size * (hop + 1)) for hop, array in enumerate(other)])
    keep, send = add_parts(keep, swap(send, "exp", 1), [owns[-1]])
    input_grad = add_parts(keep, swap(send, "exp", 2))

    hops = [[hop] for hop in range(experts)]
    placed = []
    for members in (slice(0, heads - 1), slice(heads - 1, heads)):
        own, *parts = add_partials(owns[members], others[members], hops)
        placed.append([own] + [swap(part, "exp", hop + 1) for hop, part in enumerate(parts)])
    weight_grad = place_weight_grad(placed, place, expert_weight.shape[2])
    return gradient_of_queries, gradient_of_keys, value_grad, input_grad, weight_grad


def solution(mesh):
    return jax.shard_map(
        per_device,
        mesh=mesh,
        in_specs=(
            P("seq", "exp"),
            P("seq", "exp"),
            P("seq", "exp"),
            P("seq", "exp"),
            P("seq", None),
            P("seq", None),
            P("seq", None),
            P("exp", None, None),
        ),
        out_specs=(
            P("seq", "exp"),
            P("seq", "exp"),
            P("seq", "exp"),
            P("seq", "exp"),
            P("exp", "seq", None),
        ),
        check_vma=False,
    )
```

```python
import functools

import jax
import jax.numpy as jnp
from jax import lax
from jax.experimental import pallas as pl
from jax.experimental.pallas import tpu as pltpu
from jax.sharding import PartitionSpec as P

DH = 128
PAD = 16
FIRST = 59
MIB = 1 << 20
BF16 = jnp.bfloat16
F32 = jnp.float32
VMEM = pl.BlockSpec(memory_space=pltpu.VMEM)
SMEM = pl.BlockSpec(memory_space=pltpu.SMEM)
HBM = pl.BlockSpec(memory_space=pltpu.HBM)


def struct(shape, dtype):
    return jax.ShapeDtypeStruct(shape, dtype)


TOKEN = struct((8, 128), F32)


def call(kernel, out_shape, operands, specs, wait=(), limit=16, cost=0, **options):
    known = len(operands)

    def body(*refs):
        kernel(*refs[:known], *refs[known + len(wait) :])

    grid = options.pop("grid", ())
    out_specs = options.pop("out_specs", VMEM)
    scratch = options.pop("scratch_shapes", ())
    prefetch = options.pop("prefetch", 0)
    if out_specs is VMEM and isinstance(out_shape, (list, tuple)):
        out_specs = [VMEM] * len(out_shape)
    return pl.pallas_call(
        body,
        out_shape=out_shape,
        grid_spec=pltpu.PrefetchScalarGridSpec(
            num_scalar_prefetch=prefetch,
            grid=grid,
            in_specs=list(specs) + [pl.BlockSpec(memory_space=pl.ANY)] * len(wait),
            out_specs=out_specs,
            scratch_shapes=scratch,
        ),
        cost_estimate=pl.CostEstimate(flops=cost, bytes_accessed=0, transcendentals=0),
        compiler_params=pltpu.CompilerParams(vmem_limit_bytes=limit * MIB),
        **options,
    )(*operands, *wait)


def swap(array, axis, mask):
    count = lax.axis_size(axis)
    return lax.ppermute(array, axis, [(place, place ^ mask) for place in range(count)])


def shift(array, axis, step):
    count = lax.axis_size(axis)
    return lax.ppermute(array, axis, [(place, (place + step) % count) for place in range(count)])


def dot(a, b, left, right):
    return lax.dot_general(a, b, (((left,), (right,)), ((), ())), preferred_element_type=F32)


def head(ref, number):
    return ref[:, number * DH : (number + 1) * DH]


def after(array, *earlier):
    return lax.optimization_barrier((array, *earlier))[0]


def add_arrived(total, arrived, last, wait=()):
    def kernel(total_ref, arrived_ref, narrow_ref, *wide):
        added = total_ref[...] + arrived_ref[...].astype(F32)
        narrow_ref[...] = added.astype(BF16)
        for ref in wide:
            ref[...] = added

    shapes = [struct(total.shape, BF16)] + ([] if last else [struct(total.shape, F32)])
    sent, *total = call(kernel, shapes, (total, arrived), [VMEM] * 2, wait)
    return (total[0] if total else None), sent


def touch(wait):
    def kernel(out_ref):
        out_ref[...] = jnp.zeros_like(out_ref)

    return call(kernel, TOKEN, (), (), wait)


def stack(first, second, at, wait=()):
    def kernel(a_ref, b_ref, out_ref):
        for place, ref in enumerate((a_ref, b_ref)):
            out_ref[place] = ref[...] if at[place] is None else ref[at[place]]

    return call(kernel, struct((2, *first.shape[-2:]), first.dtype), (first, second), [VMEM] * 2, wait)


def gathered_state(place, refs, number, backward):
    state = None
    for step, ref in enumerate(refs):
        lower = ((place >> step) & 1) == 0
        term = jnp.where(lower == backward, ref[number].astype(F32), 0.0)
        state = term if state is None else state + term
    return state


def triangle(size, lower):
    down = lax.broadcasted_iota(jnp.int32, (size, size), 0)
    across = lax.broadcasted_iota(jnp.int32, (size, size), 1)
    return down >= across if lower else down <= across


def intra_keys_values(query, key, value, grad, first, many, wait=()):
    rows = query.shape[0]
    tile = rows // 2

    def kernel(q_ref, k_ref, v_ref, g_ref, out_ref):
        keep = triangle(tile, False)
        for number in range(many):
            q, k, v, g = (head(ref, first + number) for ref in (q_ref, k_ref, v_ref, g_ref))
            for down in range(2):
                here = slice(down * tile, (down + 1) * tile)
                rest = slice(down * tile, rows)
                for left, right, other, place in ((v, g, q, 0), (k, q, g, DH)):
                    scores = dot(left[here], right[rest], 1, 1)
                    kept = jnp.where(keep, scores[:, :tile], 0.0).astype(BF16)
                    if down == 0:
                        kept = jnp.concatenate([kept, scores[:, tile:].astype(BF16)], axis=1)
                    out_ref[number, here, place : place + DH] = dot(kept, other[rest], 1, 0)

    return call(
        kernel,
        struct((many, rows, 2 * DH), F32),
        (query, key, value, grad),
        [VMEM] * 4,
        wait,
        cost=24 * rows * rows * many * DH,
    )


def halves(state):
    high = state.astype(BF16)
    return high, (state - high.astype(F32)).astype(BF16)


def finish_keys_values(intra, key, value, arrived, place, sets, known=(), wait=()):
    where = [(array, at) for array in range(len(intra)) for at in range(intra[array].shape[0])]
    rows, wide = intra[0].shape[1:]
    needed = sorted({start + at for start, many in sets for at in range(many or 1)})

    def kernel(place_ref, k_ref, v_ref, *refs):
        states, refs = refs[: len(arrived)], refs[len(arrived) :]
        intra_refs, refs = refs[: len(intra)], refs[len(intra) :]
        known_refs, outs = refs[: len(known)], refs[len(known) :]
        for number in needed:
            if number < len(known):
                both = known_refs[number][...]
            else:
                high, low = halves(gathered_state(place_ref[0], states, number, True))
                v, k = head(v_ref, number), head(k_ref, number)
                by_key = dot(v, high, 1, 1) + dot(v, low, 1, 1)
                by_value = dot(k, high, 1, 0) + dot(k, low, 1, 0)
                array, at = where[number]
                both = intra_refs[array][at] + jnp.concatenate([by_key, by_value], axis=1)
                both = both.astype(BF16)
            for out, (start, many) in zip(outs, sets):
                if many is None and number == start:
                    out[...] = both
                elif many is not None and start <= number < start + many:
                    out[number - start] = both

    shapes = [struct((rows, wide) if many is None else (many, rows, wide), BF16) for _, many in sets]
    operands = (place, key, value, *arrived, *intra, *known)
    return call(kernel, shapes, operands, [SMEM] + [VMEM] * (len(operands) - 1), wait)


def intra_queries(key, value, grad, wait=()):
    rows, width = key.shape
    heads = width // DH
    tile = rows // 2

    def kernel(k_ref, v_ref, g_ref, out_ref):
        keep = triangle(tile, True)
        for number in range(heads):
            k, v, grad_of = head(k_ref, number), head(v_ref, number), head(g_ref, number)
            for down in range(2):
                upto = (down + 1) * tile
                g = grad_of[down * tile : upto]
                scores = dot(g, v[:upto], 1, 1)
                last = jnp.where(keep, scores[:, down * tile :], 0.0).astype(BF16)
                if down:
                    last = jnp.concatenate([scores[:, :tile].astype(BF16), last], axis=1)
                out_ref[down * tile : upto, number * DH : (number + 1) * DH] = dot(last, k[:upto], 1, 0)

    return call(
        kernel,
        struct((rows, width), F32),
        (key, value, grad),
        [VMEM] * 3,
        wait,
        cost=24 * rows * rows * width,
    )


def finish_queries(intra, grad, arrived, place, wait=()):
    rows, width = grad.shape
    heads = width // DH

    def kernel(place_ref, intra_ref, g_ref, *refs):
        out_ref, done, sems = refs[len(arrived) :]
        copies = []
        for number in range(heads):
            high, low = halves(gathered_state(place_ref[0], refs[: len(arrived)], number, False))
            columns = slice(number * DH, (number + 1) * DH)
            g = g_ref[:, columns]
            done[number] = (intra_ref[:, columns] + dot(g, high, 1, 1) + dot(g, low, 1, 1)).astype(BF16)
            copies.append(pltpu.make_async_copy(done.at[number], out_ref.at[:, columns], sems.at[number]))
            copies[-1].start()
        for copy in copies:
            copy.wait()

    return call(
        kernel,
        struct((rows, width), BF16),
        (place, intra, grad, *arrived),
        [SMEM] + [VMEM] * (2 + len(arrived)),
        wait,
        out_specs=HBM,
        scratch_shapes=[pltpu.VMEM((heads, rows, DH), BF16), pltpu.SemaphoreType.DMA((heads,))],
    )


def place_of():
    return jnp.stack([lax.axis_index("seq"), lax.axis_index("exp")]).astype(jnp.int32)


def begin(query, grad, inputs, ids, gates, place, size, experts, count):
    rows, width = query.shape
    wide = inputs.shape[1]
    heads = width // DH
    groups = count // size
    deep = wide // count
    half = rows // 2
    tall = groups * deep + PAD

    def kernel(place_ref, *refs):
        sources, refs = refs[:5], refs[5:]
        sent_ref, refs = refs[0], refs[1:]
        outs, column_ref, refs = refs[:size], refs[size], refs[size + 1 :]
        held, sems, turned = refs[:5], refs[5], refs[6]
        copies = [
            pltpu.make_async_copy(source, target, sems.at[at])
            for at, (source, target) in enumerate(zip(sources, held))
        ]
        for copy in copies:
            copy.start()
        q_ref, g_ref, x_ref, id_ref, gate_ref = held
        copies[0].wait()
        copies[1].wait()
        for number in range(heads):
            sent_ref[number] = dot(head(q_ref, number), head(g_ref, number), 0, 0).astype(BF16)
        for copy in copies[2:]:
            copy.wait()
        step = DH * 2
        for start in range(0, wide, step):
            turned[start : start + step, :] = x_ref[:, start : start + step].astype(F32).T.astype(BF16)
        which = lax.broadcasted_iota(jnp.int32, (experts, rows), 0)
        weight = jnp.zeros((experts, rows), F32)
        for slot in range(ids.shape[0]):
            weight += jnp.where(id_ref[slot : slot + 1, :] == which, gate_ref[slot : slot + 1, :], 0.0)
        mine = jnp.sum(jnp.where(which == place_ref[1], weight, 0.0), axis=0, keepdims=True)
        column_ref[...] = jnp.broadcast_to(mine, (8, rows)).T[:, :1]
        parts = []
        for _ in range(3):
            part = weight.astype(BF16).astype(F32)
            parts.append(part)
            weight = weight - part
        tail = PAD - 3 * experts
        if tail:
            parts.append(jnp.zeros((tail, rows), F32))
        packed = jnp.concatenate(parts, axis=0)
        me = place_ref[0]
        odd = place_ref[1] & 1
        group, low = me // size, me % size
        columns = pl.ds(pl.multiple_of(odd * half, half), half)
        side = jnp.where(odd == 1, packed[:, half:], packed[:, :half]).astype(BF16)
        for member in range(size):
            for hop in range(groups):
                block = lax.rem(group + hop, groups) * size + (low ^ member)
                source = pl.ds(pl.multiple_of(block * deep, deep), deep)
                part = turned[source, columns] if member else turned[source, :]
                outs[member][hop * deep : (hop + 1) * deep, :] = part
            outs[member][groups * deep :, :] = side if member else packed.astype(BF16)

    messages = [struct((tall, half if member else rows), BF16) for member in range(size)]
    return call(
        kernel,
        [struct((heads, DH, DH), BF16)] + messages + [struct((rows, 1), F32)],
        (place, query, grad, inputs, ids, gates),
        [SMEM] + [HBM] * 5,
        limit=FIRST,
        cost=12 * rows * width * DH,
        scratch_shapes=[pltpu.VMEM((rows, width), BF16)] * 2
        + [
            pltpu.VMEM((rows, wide), BF16),
            pltpu.VMEM(ids.shape, jnp.int32),
            pltpu.VMEM(gates.shape, F32),
            pltpu.SemaphoreType.DMA((5,)),
            pltpu.VMEM((wide, rows), BF16),
        ],
    )


def own_states(first, second, arrived=None, last=False, wait=()):
    rows, width = first.shape
    heads = width // DH
    extra = [] if arrived is None else [arrived]

    def kernel(a_ref, b_ref, *refs):
        outs = refs[len(extra) :]
        for number in range(heads):
            state = dot(head(a_ref, number), head(b_ref, number), 0, 0)
            for ref in refs[: len(extra)]:
                state = state + ref[number].astype(F32)
            for out in outs:
                out[number] = state.astype(out.dtype)

    shapes = [struct((heads, DH, DH), BF16)] + ([] if last else [struct((heads, DH, DH), F32)])
    sent, *total = call(
        kernel,
        shapes,
        (first, second, *extra),
        [VMEM] * (2 + len(extra)),
        wait,
        cost=6 * rows * width * DH,
    )
    return (total[0] if total else None), sent


def weigh_inputs(own, halves_of, place, experts, wait=()):
    deep, rows = own.shape
    deep -= PAD
    half = rows // 2
    size = 1 + len(halves_of)
    flat = [entry for pair in halves_of for entry in pair]

    def kernel(place_ref, own_ref, *refs):
        out_ref = refs[len(flat)]
        odd = place_ref[1] & 1
        for at in range(1 + len(flat)):
            ref = own_ref if at == 0 else refs[at - 1]
            columns = ref[:deep, :].astype(F32)
            parts = ref[deep:, :].astype(F32)
            row = lax.broadcasted_iota(jnp.int32, parts.shape, 0)
            for step in range(experts):
                mine = (row < 3 * experts) & (lax.rem(row, experts) == (step ^ place_ref[1]))
                weight = jnp.sum(jnp.where(mine, parts, 0.0), axis=0, keepdims=True)
                scaled = (columns * weight).astype(BF16)
                if at == 0:
                    out_ref[step, :, :rows] = scaled
                else:
                    side = odd if at % 2 else 1 - odd
                    start = pl.multiple_of((at + 1) // 2 * rows + side * half, half)
                    out_ref[step, :, pl.ds(start, half)] = scaled

    return call(
        kernel,
        struct((experts, deep, size * rows), BF16),
        (place, own, *flat),
        [SMEM] + [VMEM] * (1 + len(flat)),
        wait,
    )


def weight_product(weighted, blocks, groups, wait=()):
    experts, deep, _ = weighted.shape
    rows, wide = blocks[0][0].shape[-2:]
    size = len(blocks)
    part = deep // groups

    def kernel(w_ref, *refs):
        outs = refs[size:]
        for expert in range(experts):
            total = None
            for member in range(size):
                left = w_ref[expert, :, member * rows : (member + 1) * rows]
                at = blocks[member][1]
                right = refs[member][...] if at is None else refs[member][at]
                term = dot(left, right, 1, 0)
                total = term if total is None else total + term
            for hop in range(groups):
                piece = total[hop * part : (hop + 1) * part]
                outs[hop][expert] = piece.astype(outs[hop].dtype)

    results = call(
        kernel,
        [struct((experts, part, wide), BF16 if hop else F32) for hop in range(groups)],
        (weighted, *[array for array, _ in blocks]),
        [VMEM] * (1 + size),
        wait,
        cost=2 * experts * deep * size * rows * wide,
    )
    return results[0], results[1:]


def add_partials(owns, others, sets, wait=()):
    experts, part, wide = owns[0].shape
    chunks = len(owns)
    flat = [ref for chunk in range(chunks) for ref in (owns[chunk], *others[chunk])]
    each = len(flat) // chunks

    def kernel(*refs):
        outs = refs[len(flat) :]
        for chunk in range(chunks):
            for out, hops in zip(outs, sets):
                for at, hop in enumerate(hops):
                    total = refs[chunk * each][hop]
                    for ref in refs[chunk * each + 1 : (chunk + 1) * each]:
                        total = total + ref[hop].astype(F32)
                    out[at, chunk] = total.astype(out.dtype)

    return call(
        kernel,
        [struct((len(hops), chunks, part, wide), BF16 if hops[0] else F32) for hops in sets],
        flat,
        [VMEM] * len(flat),
        wait,
    )


def place_weight_grad(pieces, place, width):
    experts = len(pieces[0])
    counts = [row[0].shape[1] for row in pieces]
    heads = sum(counts)
    part = pieces[0][0].shape[2]
    flat = [piece for row in pieces for piece in row]
    slots = heads * experts * 2

    def kernel(place_ref, *refs):
        out_ref, ready, sems = refs[len(flat) :]
        copies = []
        number = 0
        for at, many in enumerate(counts):
            for within in range(many):
                for hop in range(experts):
                    start = ((place_ref[1] ^ hop) * heads + number) * DH
                    for side in range(2):
                        slot = (number * experts + hop) * 2 + side
                        piece = refs[at * experts + hop][0, within, :, side * DH : (side + 1) * DH]
                        ready[slot] = piece.astype(F32)
                        columns = pl.ds(pl.multiple_of(start + side * (width // 2), DH), DH)
                        copy = pltpu.make_async_copy(
                            ready.at[slot], out_ref.at[0, :, columns], sems.at[slot]
                        )
                        copy.start()
                        copies.append(copy)
                number += 1
        for copy in copies:
            copy.wait()

    return call(
        kernel,
        struct((1, part, width), F32),
        (place, *flat),
        [SMEM] + [VMEM] * len(flat),
        out_specs=HBM,
        scratch_shapes=[pltpu.VMEM((slots, part, DH), F32), pltpu.SemaphoreType.DMA((slots,))],
    )


def place_keys_values(packs, wait=()):
    where = [(pack, at) for pack in range(len(packs)) for at in range(packs[pack].shape[0])]
    heads = len(where)
    rows = packs[0].shape[1]

    def kernel(*refs):
        outs, token_ref, sems = refs[len(packs) : len(packs) + 2], refs[len(packs) + 2], refs[len(packs) + 3]
        token_ref[...] = jnp.zeros_like(token_ref)
        copies = []
        for number, (pack, at) in enumerate(where):
            for side in range(2):
                source = refs[pack].at[at, :, side * DH : (side + 1) * DH]
                target = outs[side].at[:, number * DH : (number + 1) * DH]
                copies.append(pltpu.make_async_copy(source, target, sems.at[number * 2 + side]))
        for copy in copies:
            copy.start()
        for copy in copies:
            copy.wait()

    return call(
        kernel,
        [struct((rows, heads * DH), BF16)] * 2 + [TOKEN],
        packs,
        [VMEM] * len(packs),
        wait,
        out_specs=[HBM] * 2 + [VMEM],
        scratch_shapes=[pltpu.SemaphoreType.DMA((2 * heads,))],
    )


def input_products(pieces, expert_weight, gate, place, wait=()):
    experts = len(pieces)
    packs = len(pieces[0])
    where = [(pack, at) for pack in range(packs) for at in range(pieces[0][pack].shape[0])]
    heads = len(where)
    rows = pieces[0][0].shape[1]
    _, wide, width = expert_weight.shape
    part = wide // experts
    even = experts // 2

    def kernel(place_ref, w_ref, gate_ref, *refs):
        keep_ref, send_ref = refs[experts * packs :]
        for out in range(experts):
            taken = pl.ds(pl.multiple_of((place_ref[1] ^ out) * part, part), part)
            total = None
            for hop in range(experts):
                for number, (pack, at) in enumerate(where):
                    start = ((place_ref[1] ^ hop) * heads + number) * DH
                    sides = [
                        w_ref[0, taken, pl.ds(pl.multiple_of(start + side * (width // 2), DH), DH)]
                        for side in range(2)
                    ]
                    term = dot(refs[hop * packs + pack][at], jnp.concatenate(sides, axis=1), 1, 1)
                    total = term if total is None else total + term
            total = gate_ref[...] * total
            if out % 2:
                send_ref[out // 2] = total.astype(BF16)
            else:
                keep_ref[out // 2] = total

    flat = [piece for row in pieces for piece in row]
    return call(
        kernel,
        [struct((even, rows, part), F32), struct((even, rows, part), BF16)],
        (place, expert_weight, gate, *flat),
        [SMEM] + [VMEM] * (2 + len(flat)),
        wait,
        cost=2 * rows * wide * width,
    )


def add_parts(keep, arrived, wait=()):
    count, rows, wide = keep.shape
    half = count // 2

    def kernel(keep_ref, arrived_ref, *outs):
        for at in range(count):
            total = keep_ref[at] + arrived_ref[at].astype(F32)
            if count == 1:
                outs[0][...] = total.astype(BF16)
            else:
                outs[at // half][at % half] = total.astype(outs[at // half].dtype)

    if count == 1:
        shapes = struct((rows, wide), BF16)
    else:
        shapes = [struct((half, rows, wide), F32), struct((half, rows, wide), BF16)]
    return call(kernel, shapes, (keep, arrived), [VMEM] * 2, wait)


def per_device(query, key, value, grad, inputs, expert_ids, route_gates, expert_weight):
    width = query.shape[1]
    heads = width // DH
    experts = lax.axis_size("exp")
    count = lax.axis_size("seq")
    size = 4
    groups = count // size
    many = heads // 2
    place = place_of()

    sent, own_columns, one, two, three, gate = begin(
        query, grad, inputs, expert_ids.T, route_gates.T, place, size, experts, count
    )
    by_two, relay = swap(two, "seq", 2), swap(three, "seq", 2)
    later = [swap(sent, "seq", 1)]
    intra = [intra_keys_values(query, key, value, grad, 0, many)]
    total, sent = own_states(query, grad, later[0], count == 4, [relay, intra[0]])
    later.append(swap(sent, "seq", 2))
    other_total, other_sent = own_states(key, value, None, False, [sent])
    earlier = [swap(other_sent, "seq", 1)]
    intra.append(intra_keys_values(query, key, value, grad, many, heads - many, [other_sent]))
    mask = 4
    waits = [intra[-1]]
    while mask < count:
        total, sent = add_arrived(total, later[-1], 2 * mask >= count, waits)
        later.append(swap(sent, "seq", mask))
        waits = []
        mask *= 2
    other_total, other_sent = add_arrived(other_total, earlier[0], False, [sent])
    halves_of = [swap(one, "seq", 1), by_two, swap(relay, "seq", 1)]
    arrived = touch(halves_of)
    halves_of = [[half, swap(half, "exp", 1)] for half in halves_of]

    (lead,) = finish_keys_values(intra, key, value, later, place, [(0, None)], (), [other_sent, arrived])
    near = [(swap(lead, "seq", 1), None)]
    across = [(swap(lead, "seq", 2), None)]
    front, second, rest = finish_keys_values(
        intra, key, value, later, place, [(0, 2), (1, None), (2, heads - 2)], (lead,)
    )
    packs = [front, rest]
    weighted = weigh_inputs(own_columns, halves_of, place, experts, [front])
    own_heads = [(front, 0), (front, 1)] + [(rest, at) for at in range(heads - 2)]
    across.append((swap(second, "seq", 2), None))
    rest_across = swap(rest, "seq", 2)
    across += [(rest_across, at) for at in range(heads - 2)]
    far = [swap(pack, "exp", 2) for pack in packs]
    close = [swap(pack, "exp", 1) for pack in packs]
    pieces = [packs, close, far, [swap(pack, "exp", 1) for pack in far]]
    relayed = [(swap(after(across[0][0], near[0][0], weighted), "seq", 1), None)]
    owns, others = [], []
    fillers = []
    for number in range(heads):
        if number:
            waits = [owns[number - 1]]
            if number >= 2:
                waits.append(touch(others[number - 2] + [owns[number - 1]]))
            (mine, at), (came, came_at) = own_heads[number], across[number]
            stacked = stack(mine, came, (at, came_at), waits)
            pair = swap(stacked, "seq", 1)
            near.append((pair, 0))
            relayed.append((pair, 1))
        if number == 0:
            gradient_of_keys, value_grad, token = place_keys_values(packs, [weighted])
            fillers = [token]
        elif number == 1:
            intra_query = intra_queries(key, value, grad, [owns[0]])
            fillers = [intra_query]
        elif number == 2:
            keep, send = input_products(pieces, expert_weight, gate, place, [owns[1]])
            fillers = [send]
        elif number == 3:
            mask = 2
            while 2 * mask < count:
                earlier.append(swap(other_sent, "seq", mask))
                if 4 * mask < count:
                    other_total, other_sent = add_arrived(other_total, earlier[-1], False)
                mask *= 2
            keep, send = add_parts(keep, swap(send, "exp", 1))
            fillers = [touch(others[2]), touch([earlier[-1]]), send]
        own, other = weight_product(
            weighted, [own_heads[number], near[number], across[number], relayed[number]], groups, fillers
        )
        owns.append(own)
        others.append([shift(array, "seq", size * (hop + 1)) for hop, array in enumerate(other)])
    input_grad = add_parts(keep, swap(send, "exp", 2))
    _, other_sent = add_arrived(other_total, earlier[-1], True, [owns[3]])
    earlier.append(swap(other_sent, "seq", count // 2))
    gradient_of_queries = finish_queries(intra_query, grad, earlier, place)

    hops = [[hop] for hop in range(experts)]
    placed = []
    waits = []
    for members in (slice(0, heads - 1), slice(heads - 1, heads)):
        own, *parts = add_partials(owns[members], others[members], hops, waits)
        placed.append([own] + [swap(part, "exp", hop + 1) for hop, part in enumerate(parts)])
        waits = [touch(placed[0])]
    weight_grad = place_weight_grad(placed, place, expert_weight.shape[2])
    return gradient_of_queries, gradient_of_keys, value_grad, input_grad, weight_grad


def solution(mesh):
    return jax.shard_map(
        per_device,
        mesh=mesh,
        in_specs=(
            P("seq", "exp"),
            P("seq", "exp"),
            P("seq", "exp"),
            P("seq", "exp"),
            P("seq", None),
            P("seq", None),
            P("seq", None),
            P("exp", None, None),
        ),
        out_specs=(
            P("seq", "exp"),
            P("seq", "exp"),
            P("seq", "exp"),
            P("seq", "exp"),
            P("exp", "seq", None),
        ),
        check_vma=False,
    )
```

```python
import functools

import jax
import jax.numpy as jnp
from jax import lax
from jax.experimental import pallas as pl
from jax.experimental.pallas import tpu as pltpu
from jax.sharding import PartitionSpec as P

DH = 128
PAD = 16
FIRST = 60.25
MIB = 1 << 20
BF16 = jnp.bfloat16
F32 = jnp.float32
VMEM = pl.BlockSpec(memory_space=pltpu.VMEM)
SMEM = pl.BlockSpec(memory_space=pltpu.SMEM)
HBM = pl.BlockSpec(memory_space=pltpu.HBM)


def struct(shape, dtype):
    return jax.ShapeDtypeStruct(shape, dtype)


TOKEN = struct((8, 128), F32)


def call(kernel, out_shape, operands, specs, wait=(), limit=16, cost=0, **options):
    known = len(operands)

    def body(*refs):
        kernel(*refs[:known], *refs[known + len(wait) :])

    grid = options.pop("grid", ())
    out_specs = options.pop("out_specs", VMEM)
    scratch = options.pop("scratch_shapes", ())
    prefetch = options.pop("prefetch", 0)
    if out_specs is VMEM and isinstance(out_shape, (list, tuple)):
        out_specs = [VMEM] * len(out_shape)
    return pl.pallas_call(
        body,
        out_shape=out_shape,
        grid_spec=pltpu.PrefetchScalarGridSpec(
            num_scalar_prefetch=prefetch,
            grid=grid,
            in_specs=list(specs) + [pl.BlockSpec(memory_space=pl.ANY)] * len(wait),
            out_specs=out_specs,
            scratch_shapes=scratch,
        ),
        cost_estimate=pl.CostEstimate(flops=cost, bytes_accessed=0, transcendentals=0),
        compiler_params=pltpu.CompilerParams(vmem_limit_bytes=int(limit * MIB)),
        **options,
    )(*operands, *wait)


def swap(array, axis, mask):
    count = lax.axis_size(axis)
    return lax.ppermute(array, axis, [(place, place ^ mask) for place in range(count)])


def shift(array, axis, step):
    count = lax.axis_size(axis)
    return lax.ppermute(array, axis, [(place, (place + step) % count) for place in range(count)])


def dot(a, b, left, right):
    return lax.dot_general(a, b, (((left,), (right,)), ((), ())), preferred_element_type=F32)


def head(ref, number):
    return ref[:, number * DH : (number + 1) * DH]


def after(array, *earlier):
    return lax.optimization_barrier((array, *earlier))[0]


def add_arrived(total, arrived, wait=()):
    def kernel(total_ref, arrived_ref, wide_ref, narrow_ref):
        added = total_ref[...].astype(F32) + arrived_ref[...].astype(F32)
        wide_ref[...] = added
        narrow_ref[...] = added.astype(BF16)

    shapes = [struct(total.shape, F32), struct(total.shape, BF16)]
    return call(kernel, shapes, (total, arrived), [VMEM] * 2, wait)


def touch(wait):
    def kernel(out_ref):
        out_ref[...] = jnp.zeros_like(out_ref)

    return call(kernel, TOKEN, (), (), wait)


def stack(first, second, at, wait=()):
    def kernel(a_ref, b_ref, out_ref):
        for place, ref in enumerate((a_ref, b_ref)):
            out_ref[place] = ref[...] if at[place] is None else ref[at[place]]

    return call(kernel, struct((2, *first.shape[-2:]), first.dtype), (first, second), [VMEM] * 2, wait)


def last_states(total, arrived, own, wait=()):
    def kernel(total_ref, arrived_ref, own_ref, out_ref):
        half = lax.axis_size("seq") // 2
        added = total_ref[...].astype(F32) + arrived_ref[...].astype(F32)
        out_ref[...] = jnp.where(lax.axis_index("seq") >= half, added.astype(BF16), own_ref[...])

    return call(kernel, struct(own.shape, BF16), (total, arrived, own), [VMEM] * 3, wait)


def later_state(refs, number):
    state = None
    for step, ref in enumerate(refs):
        lower = ((lax.axis_index("seq") >> step) & 1) == 0
        term = jnp.where(lower, ref[number].astype(F32), 0.0)
        state = term if state is None else state + term
    return state


def earlier_state(came_ref, refs, number):
    state = None
    half = came_ref[number].astype(F32)
    for step, ref in enumerate(refs):
        upper = ((lax.axis_index("seq") >> step) & 1) == 1
        term = jnp.where(upper, ref[0, number].astype(F32), 0.0)
        state = term if state is None else state + term
        half = half + ref[1, number].astype(F32)
    return state + jnp.where(lax.axis_index("seq") >= lax.axis_size("seq") // 2, half, 0.0)


def add_both(first, second, wait=()):
    def kernel(*refs):
        for at in range(2):
            for out in refs[2:]:
                out[at] = refs[at][...].astype(out.dtype)

    shape = (2, *first.shape)
    return call(kernel, [struct(shape, F32), struct(shape, BF16)], (first, second), [VMEM] * 2, wait)


def triangle(size, lower):
    down = lax.broadcasted_iota(jnp.int32, (size, size), 0)
    across = lax.broadcasted_iota(jnp.int32, (size, size), 1)
    return down >= across if lower else down <= across


def intra_keys_values(query, key, value, grad, first, many, wait=()):
    rows = query.shape[0]
    tile = rows // 2

    def kernel(q_ref, k_ref, v_ref, g_ref, out_ref):
        keep = triangle(tile, False)
        for number in range(many):
            q, k, v, g = (head(ref, first + number) for ref in (q_ref, k_ref, v_ref, g_ref))
            for down in range(2):
                here = slice(down * tile, (down + 1) * tile)
                rest = slice(down * tile, rows)
                for left, right, other, place in ((v, g, q, 0), (k, q, g, DH)):
                    scores = dot(left[here], right[rest], 1, 1)
                    kept = jnp.where(keep, scores[:, :tile], 0.0).astype(BF16)
                    if down == 0:
                        kept = jnp.concatenate([kept, scores[:, tile:].astype(BF16)], axis=1)
                    out_ref[number, here, place : place + DH] = dot(kept, other[rest], 1, 0)

    return call(
        kernel,
        struct((many, rows, 2 * DH), F32),
        (query, key, value, grad),
        [VMEM] * 4,
        wait,
        cost=24 * rows * rows * many * DH,
    )


def halves(state):
    high = state.astype(BF16)
    return high, (state - high.astype(F32)).astype(BF16)


def finish_keys_values(intra, key, value, arrived, sets, known=(), wait=()):
    where = [(array, at) for array in range(len(intra)) for at in range(intra[array].shape[0])]
    rows, wide = intra[0].shape[1:]
    needed = sorted({start + at for start, many in sets for at in range(many or 1)})

    def kernel(k_ref, v_ref, *refs):
        states, refs = refs[: len(arrived)], refs[len(arrived) :]
        intra_refs, refs = refs[: len(intra)], refs[len(intra) :]
        known_refs, outs = refs[: len(known)], refs[len(known) :]
        for number in needed:
            if number < len(known):
                both = known_refs[number][...]
            else:
                high, low = halves(later_state(states, number))
                v, k = head(v_ref, number), head(k_ref, number)
                by_key = dot(v, high, 1, 1) + dot(v, low, 1, 1)
                by_value = dot(k, high, 1, 0) + dot(k, low, 1, 0)
                array, at = where[number]
                both = intra_refs[array][at] + jnp.concatenate([by_key, by_value], axis=1)
                both = both.astype(BF16)
            for out, (start, many) in zip(outs, sets):
                if many is None and number == start:
                    out[...] = both
                elif many is not None and start <= number < start + many:
                    out[number - start] = both

    shapes = [struct((rows, wide) if many is None else (many, rows, wide), BF16) for _, many in sets]
    operands = (key, value, *arrived, *intra, *known)
    return call(kernel, shapes, operands, [VMEM] * len(operands), wait)


def intra_queries(key, value, grad, wait=()):
    rows, width = key.shape
    heads = width // DH
    tile = rows // 2

    def kernel(k_ref, v_ref, g_ref, out_ref):
        keep = triangle(tile, True)
        for number in range(heads):
            k, v, grad_of = head(k_ref, number), head(v_ref, number), head(g_ref, number)
            for down in range(2):
                upto = (down + 1) * tile
                g = grad_of[down * tile : upto]
                scores = dot(g, v[:upto], 1, 1)
                last = jnp.where(keep, scores[:, down * tile :], 0.0).astype(BF16)
                if down:
                    last = jnp.concatenate([scores[:, :tile].astype(BF16), last], axis=1)
                out_ref[down * tile : upto, number * DH : (number + 1) * DH] = dot(last, k[:upto], 1, 0)

    return call(
        kernel,
        struct((rows, width), F32),
        (key, value, grad),
        [VMEM] * 3,
        wait,
        cost=24 * rows * rows * width,
    )


def finish_queries(intra, grad, came, arrived, wait=()):
    rows, width = grad.shape
    heads = width // DH

    def kernel(intra_ref, g_ref, came_ref, *refs):
        out_ref, done, sems = refs[len(arrived) :]
        copies = []
        for number in range(heads):
            high, low = halves(earlier_state(came_ref, refs[: len(arrived)], number))
            columns = slice(number * DH, (number + 1) * DH)
            g = g_ref[:, columns]
            done[number] = (intra_ref[:, columns] + dot(g, high, 1, 1) + dot(g, low, 1, 1)).astype(BF16)
            copies.append(pltpu.make_async_copy(done.at[number], out_ref.at[:, columns], sems.at[number]))
            copies[-1].start()
        for copy in copies:
            copy.wait()

    return call(
        kernel,
        struct((rows, width), BF16),
        (intra, grad, came, *arrived),
        [VMEM] * (3 + len(arrived)),
        wait,
        out_specs=HBM,
        scratch_shapes=[pltpu.VMEM((heads, rows, DH), BF16), pltpu.SemaphoreType.DMA((heads,))],
    )


def begin(query, grad, inputs, ids, gates, size, experts, count):
    rows, width = query.shape
    wide = inputs.shape[1]
    heads = width // DH
    groups = count // size
    deep = wide // count
    half = rows // 2
    tall = groups * deep + PAD

    def kernel(*refs):
        me, mine_at = lax.axis_index("seq"), lax.axis_index("exp")
        sources, refs = refs[:5], refs[5:]
        sent_ref, refs = refs[0], refs[1:]
        outs, column_ref, refs = refs[:size], refs[size], refs[size + 1 :]
        held, sems, turned = refs[:5], refs[5], refs[6]
        copies = [
            pltpu.make_async_copy(source, target, sems.at[at])
            for at, (source, target) in enumerate(zip(sources, held))
        ]
        for copy in copies:
            copy.start()
        q_ref, g_ref, x_ref, id_ref, gate_ref = held
        copies[0].wait()
        copies[1].wait()
        for number in range(heads):
            sent_ref[number] = dot(head(q_ref, number), head(g_ref, number), 0, 0).astype(BF16)
        for copy in copies[2:]:
            copy.wait()
        step = DH * 2
        for start in range(0, wide, step):
            turned[start : start + step, :] = x_ref[:, start : start + step].astype(F32).T.astype(BF16)
        which = lax.broadcasted_iota(jnp.int32, (experts, rows), 0)
        weight = jnp.zeros((experts, rows), F32)
        for slot in range(ids.shape[0]):
            weight += jnp.where(id_ref[slot : slot + 1, :] == which, gate_ref[slot : slot + 1, :], 0.0)
        mine = jnp.sum(jnp.where(which == mine_at, weight, 0.0), axis=0, keepdims=True)
        column_ref[...] = jnp.broadcast_to(mine, (8, rows)).T[:, :1]
        parts = []
        for _ in range(3):
            part = weight.astype(BF16).astype(F32)
            parts.append(part)
            weight = weight - part
        tail = PAD - 3 * experts
        if tail:
            parts.append(jnp.zeros((tail, rows), F32))
        packed = jnp.concatenate(parts, axis=0)
        odd = mine_at & 1
        group, low = me // size, me % size
        columns = pl.ds(pl.multiple_of(odd * half, half), half)
        side = jnp.where(odd == 1, packed[:, half:], packed[:, :half]).astype(BF16)
        for member in range(size):
            for hop in range(groups):
                block = lax.rem(group + hop, groups) * size + (low ^ member)
                source = pl.ds(pl.multiple_of(block * deep, deep), deep)
                part = turned[source, columns] if member else turned[source, :]
                outs[member][hop * deep : (hop + 1) * deep, :] = part
            outs[member][groups * deep :, :] = side if member else packed.astype(BF16)

    messages = [struct((tall, half if member else rows), BF16) for member in range(size)]
    return call(
        kernel,
        [struct((heads, DH, DH), BF16)] + messages + [struct((rows, 1), F32)],
        (query, grad, inputs, ids, gates),
        [HBM] * 5,
        limit=FIRST,
        cost=12 * rows * width * DH,
        scratch_shapes=[pltpu.VMEM((rows, width), BF16)] * 2
        + [
            pltpu.VMEM((rows, wide), BF16),
            pltpu.VMEM(ids.shape, jnp.int32),
            pltpu.VMEM(gates.shape, F32),
            pltpu.SemaphoreType.DMA((5,)),
            pltpu.VMEM((wide, rows), BF16),
        ],
    )


def own_states(first, second):
    rows, width = first.shape
    heads = width // DH

    def kernel(a_ref, b_ref, out_ref):
        for number in range(heads):
            out_ref[number] = dot(head(a_ref, number), head(b_ref, number), 0, 0).astype(BF16)

    shape = struct((heads, DH, DH), BF16)
    return call(kernel, shape, (first, second), [VMEM] * 2, cost=6 * rows * width * DH)


def weigh_inputs(own, halves_of, experts, wait=()):
    deep, rows = own.shape
    deep -= PAD
    half = rows // 2
    size = 1 + len(halves_of)
    flat = [entry for pair in halves_of for entry in pair]

    def kernel(own_ref, *refs):
        out_ref = refs[len(flat)]
        odd = lax.axis_index("exp") & 1
        for at in range(1 + len(flat)):
            ref = own_ref if at == 0 else refs[at - 1]
            columns = ref[:deep, :].astype(F32)
            parts = ref[deep:, :].astype(F32)
            row = lax.broadcasted_iota(jnp.int32, parts.shape, 0)
            for step in range(experts):
                mine = (row < 3 * experts) & (lax.rem(row, experts) == (step ^ lax.axis_index("exp")))
                weight = jnp.sum(jnp.where(mine, parts, 0.0), axis=0, keepdims=True)
                scaled = (columns * weight).astype(BF16)
                if at == 0:
                    out_ref[step, :, :rows] = scaled
                else:
                    side = odd if at % 2 else 1 - odd
                    start = pl.multiple_of((at + 1) // 2 * rows + side * half, half)
                    out_ref[step, :, pl.ds(start, half)] = scaled

    return call(
        kernel,
        struct((experts, deep, size * rows), BF16),
        (own, *flat),
        [VMEM] * (1 + len(flat)),
        wait,
    )


def weight_product(weighted, blocks, groups, wait=()):
    experts, deep, _ = weighted.shape
    rows, wide = blocks[0][0].shape[-2:]
    size = len(blocks)
    part = deep // groups

    def kernel(w_ref, *refs):
        outs = refs[size:]
        for expert in range(experts):
            total = None
            for member in range(size):
                left = w_ref[expert, :, member * rows : (member + 1) * rows]
                at = blocks[member][1]
                right = refs[member][...] if at is None else refs[member][at]
                term = dot(left, right, 1, 0)
                total = term if total is None else total + term
            for hop in range(groups):
                piece = total[hop * part : (hop + 1) * part]
                outs[hop][expert] = piece.astype(outs[hop].dtype)

    results = call(
        kernel,
        [struct((experts, part, wide), BF16 if hop else F32) for hop in range(groups)],
        (weighted, *[array for array, _ in blocks]),
        [VMEM] * (1 + size),
        wait,
        cost=2 * experts * deep * size * rows * wide,
    )
    return results[0], results[1:]


def add_partials(owns, others, sets, wait=()):
    experts, part, wide = owns[0].shape
    chunks = len(owns)
    flat = [ref for chunk in range(chunks) for ref in (owns[chunk], *others[chunk])]
    each = len(flat) // chunks

    def kernel(*refs):
        outs = refs[len(flat) :]
        for chunk in range(chunks):
            for out, hops in zip(outs, sets):
                for at, hop in enumerate(hops):
                    total = refs[chunk * each][hop]
                    for ref in refs[chunk * each + 1 : (chunk + 1) * each]:
                        total = total + ref[hop].astype(F32)
                    out[at, chunk] = total.astype(out.dtype)

    return call(
        kernel,
        [struct((len(hops), chunks, part, wide), BF16 if hops[0] else F32) for hops in sets],
        flat,
        [VMEM] * len(flat),
        wait,
    )


def place_weight_grad(pieces, width, first, heads, before=None, wait=()):
    experts = len(pieces)
    _, many, part, _ = pieces[0].shape
    extra = [] if before is None else [before]
    slots = many * experts * 2

    def kernel(*refs):
        out_ref, token_ref, ready, sems = refs[experts + len(extra) :]
        token_ref[...] = jnp.zeros_like(token_ref)
        copies = []
        for number in range(many):
            for hop in range(experts):
                start = ((lax.axis_index("exp") ^ hop) * heads + first + number) * DH
                for side in range(2):
                    slot = (number * experts + hop) * 2 + side
                    ready[slot] = refs[hop][0, number, :, side * DH : (side + 1) * DH].astype(F32)
                    columns = pl.ds(pl.multiple_of(start + side * (width // 2), DH), DH)
                    copy = pltpu.make_async_copy(ready.at[slot], out_ref.at[0, :, columns], sems.at[slot])
                    copy.start()
                    copies.append(copy)
        for copy in copies:
            copy.wait()

    return call(
        kernel,
        [struct((1, part, width), F32), TOKEN],
        (*pieces, *extra),
        [VMEM] * experts + [HBM] * len(extra),
        wait,
        out_specs=[HBM, VMEM],
        scratch_shapes=[pltpu.VMEM((slots, part, DH), F32), pltpu.SemaphoreType.DMA((slots,))],
        input_output_aliases={experts: 0} if extra else {},
    )


def place_keys_values(packs, wait=()):
    where = [(pack, at) for pack in range(len(packs)) for at in range(packs[pack].shape[0])]
    heads = len(where)
    rows = packs[0].shape[1]

    def kernel(*refs):
        outs, token_ref, sems = refs[len(packs) : len(packs) + 2], refs[len(packs) + 2], refs[len(packs) + 3]
        token_ref[...] = jnp.zeros_like(token_ref)
        copies = []
        for number, (pack, at) in enumerate(where):
            for side in range(2):
                source = refs[pack].at[at, :, side * DH : (side + 1) * DH]
                target = outs[side].at[:, number * DH : (number + 1) * DH]
                copies.append(pltpu.make_async_copy(source, target, sems.at[number * 2 + side]))
        for copy in copies:
            copy.start()
        for copy in copies:
            copy.wait()

    return call(
        kernel,
        [struct((rows, heads * DH), BF16)] * 2 + [TOKEN],
        packs,
        [VMEM] * len(packs),
        wait,
        out_specs=[HBM] * 2 + [VMEM],
        scratch_shapes=[pltpu.SemaphoreType.DMA((2 * heads,))],
    )


def input_products(pieces, expert_weight, gate, wait=()):
    experts = len(pieces)
    packs = len(pieces[0])
    where = [(pack, at) for pack in range(packs) for at in range(pieces[0][pack].shape[0])]
    heads = len(where)
    rows = pieces[0][0].shape[1]
    _, wide, width = expert_weight.shape
    part = wide // experts
    even = experts // 2

    def kernel(w_ref, gate_ref, *refs):
        keep_ref, *send_refs = refs[experts * packs :]
        for out in range(experts):
            taken = pl.ds(pl.multiple_of((lax.axis_index("exp") ^ out) * part, part), part)
            total = None
            for hop in range(experts):
                for number, (pack, at) in enumerate(where):
                    start = ((lax.axis_index("exp") ^ hop) * heads + number) * DH
                    sides = [
                        w_ref[0, taken, pl.ds(pl.multiple_of(start + side * (width // 2), DH), DH)]
                        for side in range(2)
                    ]
                    term = dot(refs[hop * packs + pack][at], jnp.concatenate(sides, axis=1), 1, 1)
                    total = term if total is None else total + term
            total = gate_ref[...] * total
            if out % 2:
                send_refs[out // 2][...] = total.astype(BF16)
            else:
                keep_ref[out // 2] = total

    flat = [piece for row in pieces for piece in row]
    return call(
        kernel,
        [struct((even, rows, part), F32)] + [struct((rows, part), BF16)] * even,
        (expert_weight, gate, *flat),
        [VMEM] * (2 + len(flat)),
        wait,
        cost=2 * rows * wide * width,
    )


def add_parts(keep, arrived, wait=()):
    count, rows, wide = keep.shape
    half = count // 2

    def kernel(keep_ref, *refs):
        arrived_refs, outs = refs[:count], refs[count:]
        if not half:
            outs[1][...] = jnp.zeros_like(outs[1])
        for at in range(count):
            total = keep_ref[at] + arrived_refs[at][...].astype(F32)
            if at < half:
                outs[0][at] = total
            else:
                outs[at - half + min(half, 1)][...] = total.astype(BF16)

    if half:
        shapes = [struct((half, rows, wide), F32)] + [struct((rows, wide), BF16)] * (count - half)
    else:
        shapes = [struct((rows, wide), BF16), TOKEN]
    return call(kernel, shapes, (keep, *arrived), [VMEM] * (1 + count), wait)


def per_device(query, key, value, grad, inputs, expert_ids, route_gates, expert_weight):
    width = query.shape[1]
    heads = width // DH
    experts = lax.axis_size("exp")
    count = lax.axis_size("seq")
    size = 4
    groups = count // size
    many = heads // 2

    sent, own_columns, one, two, three, gate = begin(
        query, grad, inputs, expert_ids.T, route_gates.T, size, experts, count
    )
    by_two, relay = swap(two, "seq", 2), swap(three, "seq", 2)
    later = [swap(sent, "seq", 1)]
    other_state = own_states(key, value)
    total, sent = add_arrived(sent, later[0], [other_state])
    later.append(swap(sent, "seq", 2))
    mask = 4
    while 2 * mask < count:
        total, sent = add_arrived(total, later[-1])
        later.append(swap(sent, "seq", mask))
        mask *= 2
    sent = last_states(total, later[-1], other_state, [relay])
    came = swap(sent, "seq", mask)
    later.append(came)
    intra = [intra_keys_values(query, key, value, grad, 0, many, [sent])]
    intra.append(intra_keys_values(query, key, value, grad, many, heads - many, [intra[0]]))
    halves_of = [swap(one, "seq", 1), by_two, swap(relay, "seq", 1)]
    arrived = touch(halves_of)
    halves_of = [[half, swap(half, "exp", 1)] for half in halves_of]

    (lead,) = finish_keys_values(intra, key, value, later, [(0, None)], (), [intra[1], arrived])
    near = [(swap(lead, "seq", 1), None)]
    across = [(swap(lead, "seq", 2), None)]
    every, second, rest = finish_keys_values(
        intra, key, value, later, [(0, heads), (1, None), (2, heads - 2)], (lead,), [pair[1] for pair in halves_of]
    )
    packs = [every]
    weighted = weigh_inputs(own_columns, halves_of, experts)
    own_heads = [(every, at) for at in range(heads)]
    across.append((swap(second, "seq", 2), None))
    rest_across = swap(rest, "seq", 2)
    across += [(rest_across, at) for at in range(heads - 2)]
    far = [swap(pack, "exp", 2) for pack in packs]
    close = [swap(pack, "exp", 1) for pack in packs]
    pieces = [packs, close, far, [swap(pack, "exp", 1) for pack in far]]
    relayed = [(swap(after(across[0][0], near[0][0], weighted), "seq", 1), None)]
    owns, others = [], []
    fillers = []
    for number in range(heads):
        if number:
            waits = [owns[number - 1]]
            if number >= 2:
                waits.append(touch(others[number - 2] + [owns[number - 1]]))
            (mine, at), (passed, passed_at) = own_heads[number], across[number]
            stacked = stack(mine, passed, (at, passed_at), waits)
            pair = swap(stacked, "seq", 1)
            near.append((pair, 0))
            relayed.append((pair, 1))
        if number == 0:
            gradient_of_keys, value_grad, token = place_keys_values(packs, [weighted])
            fillers = [token]
        elif number == 1:
            intra_query = intra_queries(key, value, grad, [owns[0]])
            fillers = [intra_query]
        elif number == 2:
            fillers = []
        elif number == 3:
            total, sent = add_both(other_state, came, [owns[2]])
            earlier = [swap(sent, "seq", 1)]
            keep, *send = input_products(pieces, expert_weight, gate, [owns[2]])
            fillers = [touch(others[2]), send[0]]
        own, other = weight_product(
            weighted, [own_heads[number], near[number], across[number], relayed[number]], groups, fillers
        )
        owns.append(own)
        others.append([shift(array, "seq", size * (hop + 1)) for hop, array in enumerate(other)])
    mask = 1
    while keep.ndim == 3:
        keep, *send = add_parts(keep, [swap(part, "exp", mask) for part in send])
        mask *= 2
    input_grad, input_token = keep, send[0]
    mask = 2
    while 2 * mask < count:
        total, sent = add_arrived(total, earlier[-1])
        earlier.append(swap(sent, "seq", mask))
        mask *= 2
    gradient_of_queries = finish_queries(intra_query, grad, came, earlier)

    hops = [[hop] for hop in range(experts)]
    weight_grad = None
    waits, placing = [], []
    for first, last in ((0, heads - 1), (heads - 1, heads)):
        own, *parts = add_partials(owns[first:last], others[first:last], hops, waits)
        parts = [own] + [swap(part, "exp", hop + 1) for hop, part in enumerate(parts)]
        weight_grad, token = place_weight_grad(
            parts, expert_weight.shape[2], first, heads, weight_grad, placing
        )
        waits, placing = [token], [input_token]
    return gradient_of_queries, gradient_of_keys, value_grad, input_grad, weight_grad


def solution(mesh):
    return jax.shard_map(
        per_device,
        mesh=mesh,
        in_specs=(
            P("seq", "exp"),
            P("seq", "exp"),
            P("seq", "exp"),
            P("seq", "exp"),
            P("seq", None),
            P("seq", None),
            P("seq", None),
            P("exp", None, None),
        ),
        out_specs=(
            P("seq", "exp"),
            P("seq", "exp"),
            P("seq", "exp"),
            P("seq", "exp"),
            P("exp", "seq", None),
        ),
        check_vma=False,
    )
```

```python
import functools

import jax
import jax.numpy as jnp
from jax import lax
from jax.experimental import pallas as pl
from jax.experimental.pallas import tpu as pltpu
from jax.sharding import PartitionSpec as P

DH = 128
PAD = 16
FIRST = 60.25
MIB = 1 << 20
BF16 = jnp.bfloat16
F32 = jnp.float32
VMEM = pl.BlockSpec(memory_space=pltpu.VMEM)
SMEM = pl.BlockSpec(memory_space=pltpu.SMEM)
HBM = pl.BlockSpec(memory_space=pltpu.HBM)


def struct(shape, dtype):
    return jax.ShapeDtypeStruct(shape, dtype)


TOKEN = struct((8, 128), F32)


def call(kernel, out_shape, operands, specs, wait=(), limit=16, cost=0, **options):
    known = len(operands)

    def body(*refs):
        kernel(*refs[:known], *refs[known + len(wait) :])

    grid = options.pop("grid", ())
    out_specs = options.pop("out_specs", VMEM)
    scratch = options.pop("scratch_shapes", ())
    prefetch = options.pop("prefetch", 0)
    if out_specs is VMEM and isinstance(out_shape, (list, tuple)):
        out_specs = [VMEM] * len(out_shape)
    return pl.pallas_call(
        body,
        out_shape=out_shape,
        grid_spec=pltpu.PrefetchScalarGridSpec(
            num_scalar_prefetch=prefetch,
            grid=grid,
            in_specs=list(specs) + [pl.BlockSpec(memory_space=pl.ANY)] * len(wait),
            out_specs=out_specs,
            scratch_shapes=scratch,
        ),
        cost_estimate=pl.CostEstimate(flops=cost, bytes_accessed=0, transcendentals=0),
        compiler_params=pltpu.CompilerParams(vmem_limit_bytes=int(limit * MIB)),
        **options,
    )(*operands, *wait)


def swap(array, axis, mask):
    count = lax.axis_size(axis)
    return lax.ppermute(array, axis, [(place, place ^ mask) for place in range(count)])


def shift(array, axis, step):
    count = lax.axis_size(axis)
    return lax.ppermute(array, axis, [(place, (place + step) % count) for place in range(count)])


def dot(a, b, left, right):
    return lax.dot_general(a, b, (((left,), (right,)), ((), ())), preferred_element_type=F32)


def head(ref, number):
    return ref[:, number * DH : (number + 1) * DH]


def after(array, *earlier):
    return lax.optimization_barrier((array, *earlier))[0]


def add_arrived(total, arrived, wait=()):
    def kernel(total_ref, arrived_ref, wide_ref, narrow_ref):
        added = total_ref[...].astype(F32) + arrived_ref[...].astype(F32)
        wide_ref[...] = added
        narrow_ref[...] = added.astype(BF16)

    shapes = [struct(total.shape, F32), struct(total.shape, BF16)]
    return call(kernel, shapes, (total, arrived), [VMEM] * 2, wait)


def touch(wait):
    def kernel(out_ref):
        out_ref[...] = jnp.zeros_like(out_ref)

    return call(kernel, TOKEN, (), (), wait)


def stack(first, second, at, wait=()):
    def kernel(a_ref, b_ref, out_ref):
        for place, ref in enumerate((a_ref, b_ref)):
            out_ref[place] = ref[...] if at[place] is None else ref[at[place]]

    return call(kernel, struct((2, *first.shape[-2:]), first.dtype), (first, second), [VMEM] * 2, wait)


def last_states(total, arrived, own, wait=()):
    def kernel(total_ref, arrived_ref, own_ref, out_ref):
        half = lax.axis_size("seq") // 2
        added = total_ref[...].astype(F32) + arrived_ref[...].astype(F32)
        out_ref[...] = jnp.where(lax.axis_index("seq") >= half, added.astype(BF16), own_ref[...])

    return call(kernel, struct(own.shape, BF16), (total, arrived, own), [VMEM] * 3, wait)


def later_state(refs, number):
    state = None
    for step, ref in enumerate(refs):
        lower = ((lax.axis_index("seq") >> step) & 1) == 0
        term = jnp.where(lower, ref[number].astype(F32), 0.0)
        state = term if state is None else state + term
    return state


def earlier_state(came_ref, refs, number):
    state = None
    half = came_ref[number].astype(F32)
    for step, ref in enumerate(refs):
        upper = ((lax.axis_index("seq") >> step) & 1) == 1
        term = jnp.where(upper, ref[0, number].astype(F32), 0.0)
        state = term if state is None else state + term
        half = half + ref[1, number].astype(F32)
    return state + jnp.where(lax.axis_index("seq") >= lax.axis_size("seq") // 2, half, 0.0)


def add_both(first, second, wait=()):
    def kernel(*refs):
        for at in range(2):
            for out in refs[2:]:
                out[at] = refs[at][...].astype(out.dtype)

    shape = (2, *first.shape)
    return call(kernel, [struct(shape, F32), struct(shape, BF16)], (first, second), [VMEM] * 2, wait)


def triangle(size, lower):
    down = lax.broadcasted_iota(jnp.int32, (size, size), 0)
    across = lax.broadcasted_iota(jnp.int32, (size, size), 1)
    return down >= across if lower else down <= across


def intra_keys_values(query, key, value, grad, first, many, wait=()):
    rows = query.shape[0]
    tile = rows // 2

    def kernel(q_ref, k_ref, v_ref, g_ref, out_ref):
        keep = triangle(tile, False)
        for number in range(many):
            q, k, v, g = (head(ref, first + number) for ref in (q_ref, k_ref, v_ref, g_ref))
            for down in range(2):
                here = slice(down * tile, (down + 1) * tile)
                rest = slice(down * tile, rows)
                for left, right, other, place in ((v, g, q, 0), (k, q, g, DH)):
                    scores = dot(left[here], right[rest], 1, 1)
                    kept = jnp.where(keep, scores[:, :tile], 0.0).astype(BF16)
                    if down == 0:
                        kept = jnp.concatenate([kept, scores[:, tile:].astype(BF16)], axis=1)
                    out_ref[number, here, place : place + DH] = dot(kept, other[rest], 1, 0)

    return call(
        kernel,
        struct((many, rows, 2 * DH), F32),
        (query, key, value, grad),
        [VMEM] * 4,
        wait,
        cost=24 * rows * rows * many * DH,
    )


def halves(state):
    high = state.astype(BF16)
    return high, (state - high.astype(F32)).astype(BF16)


def finish_keys_values(intra, key, value, arrived, sets, known=(), wait=()):
    where = [(array, at) for array in range(len(intra)) for at in range(intra[array].shape[0])]
    rows, wide = intra[0].shape[1:]
    needed = sorted({start + at for start, many in sets for at in range(many or 1)})

    def kernel(k_ref, v_ref, *refs):
        states, refs = refs[: len(arrived)], refs[len(arrived) :]
        intra_refs, refs = refs[: len(intra)], refs[len(intra) :]
        known_refs, outs = refs[: len(known)], refs[len(known) :]
        for number in needed:
            if number < len(known):
                both = known_refs[number][...]
            else:
                high, low = halves(later_state(states, number))
                v, k = head(v_ref, number), head(k_ref, number)
                by_key = dot(v, high, 1, 1) + dot(v, low, 1, 1)
                by_value = dot(k, high, 1, 0) + dot(k, low, 1, 0)
                array, at = where[number]
                both = intra_refs[array][at] + jnp.concatenate([by_key, by_value], axis=1)
                both = both.astype(BF16)
            for out, (start, many) in zip(outs, sets):
                if many is None and number == start:
                    out[...] = both
                elif many is not None and start <= number < start + many:
                    out[number - start] = both

    shapes = [struct((rows, wide) if many is None else (many, rows, wide), BF16) for _, many in sets]
    operands = (key, value, *arrived, *intra, *known)
    return call(kernel, shapes, operands, [VMEM] * len(operands), wait)


def intra_queries(key, value, grad, wait=()):
    rows, width = key.shape
    heads = width // DH
    tile = rows // 2

    def kernel(k_ref, v_ref, g_ref, out_ref):
        keep = triangle(tile, True)
        for number in range(heads):
            k, v, grad_of = head(k_ref, number), head(v_ref, number), head(g_ref, number)
            for down in range(2):
                upto = (down + 1) * tile
                g = grad_of[down * tile : upto]
                scores = dot(g, v[:upto], 1, 1)
                last = jnp.where(keep, scores[:, down * tile :], 0.0).astype(BF16)
                if down:
                    last = jnp.concatenate([scores[:, :tile].astype(BF16), last], axis=1)
                out_ref[down * tile : upto, number * DH : (number + 1) * DH] = dot(last, k[:upto], 1, 0)

    return call(
        kernel,
        struct((rows, width), F32),
        (key, value, grad),
        [VMEM] * 3,
        wait,
        cost=24 * rows * rows * width,
    )


def finish_queries(intra, grad, came, arrived, wait=()):
    rows, width = grad.shape
    heads = width // DH

    def kernel(intra_ref, g_ref, came_ref, *refs):
        out_ref, done, sems = refs[len(arrived) :]
        copies = []
        for number in range(heads):
            high, low = halves(earlier_state(came_ref, refs[: len(arrived)], number))
            columns = slice(number * DH, (number + 1) * DH)
            g = g_ref[:, columns]
            done[number] = (intra_ref[:, columns] + dot(g, high, 1, 1) + dot(g, low, 1, 1)).astype(BF16)
            copies.append(pltpu.make_async_copy(done.at[number], out_ref.at[:, columns], sems.at[number]))
            copies[-1].start()
        for copy in copies:
            copy.wait()

    return call(
        kernel,
        struct((rows, width), BF16),
        (intra, grad, came, *arrived),
        [VMEM] * (3 + len(arrived)),
        wait,
        out_specs=HBM,
        scratch_shapes=[pltpu.VMEM((heads, rows, DH), BF16), pltpu.SemaphoreType.DMA((heads,))],
    )


def begin(query, grad, inputs, ids, gates, size, experts, count):
    rows, width = query.shape
    wide = inputs.shape[1]
    heads = width // DH
    groups = count // size
    deep = wide // count
    half = rows // 2
    tall = groups * deep + PAD

    def kernel(*refs):
        me, mine_at = lax.axis_index("seq"), lax.axis_index("exp")
        sources, refs = refs[:5], refs[5:]
        sent_ref, refs = refs[0], refs[1:]
        outs, column_ref, refs = refs[:size], refs[size], refs[size + 1 :]
        held, sems, turned = refs[:5], refs[5], refs[6]
        copies = [
            pltpu.make_async_copy(source, target, sems.at[at])
            for at, (source, target) in enumerate(zip(sources, held))
        ]
        for copy in copies:
            copy.start()
        q_ref, g_ref, x_ref, id_ref, gate_ref = held
        copies[0].wait()
        copies[1].wait()
        for number in range(heads):
            sent_ref[number] = dot(head(q_ref, number), head(g_ref, number), 0, 0).astype(BF16)
        for copy in copies[2:]:
            copy.wait()
        step = DH * 2
        for start in range(0, wide, step):
            turned[start : start + step, :] = x_ref[:, start : start + step].astype(F32).T.astype(BF16)
        which = lax.broadcasted_iota(jnp.int32, (experts, rows), 0)
        weight = jnp.zeros((experts, rows), F32)
        for slot in range(ids.shape[0]):
            weight += jnp.where(id_ref[slot : slot + 1, :] == which, gate_ref[slot : slot + 1, :], 0.0)
        mine = jnp.sum(jnp.where(which == mine_at, weight, 0.0), axis=0, keepdims=True)
        column_ref[...] = jnp.broadcast_to(mine, (8, rows)).T[:, :1]
        parts = []
        for _ in range(3):
            part = weight.astype(BF16).astype(F32)
            parts.append(part)
            weight = weight - part
        tail = PAD - 3 * experts
        if tail:
            parts.append(jnp.zeros((tail, rows), F32))
        packed = jnp.concatenate(parts, axis=0)
        odd = mine_at & 1
        group, low = me // size, me % size
        columns = pl.ds(pl.multiple_of(odd * half, half), half)
        side = jnp.where(odd == 1, packed[:, half:], packed[:, :half]).astype(BF16)
        for member in range(size):
            for hop in range(groups):
                block = lax.rem(group + hop, groups) * size + (low ^ member)
                source = pl.ds(pl.multiple_of(block * deep, deep), deep)
                part = turned[source, columns] if member else turned[source, :]
                outs[member][hop * deep : (hop + 1) * deep, :] = part
            outs[member][groups * deep :, :] = side if member else packed.astype(BF16)

    messages = [struct((tall, half if member else rows), BF16) for member in range(size)]
    return call(
        kernel,
        [struct((heads, DH, DH), BF16)] + messages + [struct((rows, 1), F32)],
        (query, grad, inputs, ids, gates),
        [HBM] * 5,
        limit=FIRST,
        cost=12 * rows * width * DH,
        scratch_shapes=[pltpu.VMEM((rows, width), BF16)] * 2
        + [
            pltpu.VMEM((rows, wide), BF16),
            pltpu.VMEM(ids.shape, jnp.int32),
            pltpu.VMEM(gates.shape, F32),
            pltpu.SemaphoreType.DMA((5,)),
            pltpu.VMEM((wide, rows), BF16),
        ],
    )


def own_states(first, second):
    rows, width = first.shape
    heads = width // DH

    def kernel(a_ref, b_ref, out_ref):
        for number in range(heads):
            out_ref[number] = dot(head(a_ref, number), head(b_ref, number), 0, 0).astype(BF16)

    shape = struct((heads, DH, DH), BF16)
    return call(kernel, shape, (first, second), [VMEM] * 2, cost=6 * rows * width * DH)


def weigh_inputs(own, halves_of, experts, wait=()):
    deep, rows = own.shape
    deep -= PAD
    half = rows // 2
    size = 1 + len(halves_of)
    flat = [entry for pair in halves_of for entry in pair]

    def kernel(own_ref, *refs):
        out_ref = refs[len(flat)]
        odd = lax.axis_index("exp") & 1
        for at in range(1 + len(flat)):
            ref = own_ref if at == 0 else refs[at - 1]
            columns = ref[:deep, :].astype(F32)
            parts = ref[deep:, :].astype(F32)
            row = lax.broadcasted_iota(jnp.int32, parts.shape, 0)
            for step in range(experts):
                mine = (row < 3 * experts) & (lax.rem(row, experts) == (step ^ lax.axis_index("exp")))
                weight = jnp.sum(jnp.where(mine, parts, 0.0), axis=0, keepdims=True)
                scaled = (columns * weight).astype(BF16)
                if at == 0:
                    out_ref[step, :, :rows] = scaled
                else:
                    side = odd if at % 2 else 1 - odd
                    start = pl.multiple_of((at + 1) // 2 * rows + side * half, half)
                    out_ref[step, :, pl.ds(start, half)] = scaled

    return call(
        kernel,
        struct((experts, deep, size * rows), BF16),
        (own, *flat),
        [VMEM] * (1 + len(flat)),
        wait,
    )


def weight_product(weighted, blocks, groups, wait=()):
    experts, deep, _ = weighted.shape
    rows, wide = blocks[0][0].shape[-2:]
    size = len(blocks)
    part = deep // groups

    def kernel(w_ref, *refs):
        outs = refs[size:]
        for expert in range(experts):
            total = None
            for member in range(size):
                left = w_ref[expert, :, member * rows : (member + 1) * rows]
                at = blocks[member][1]
                right = refs[member][...] if at is None else refs[member][at]
                term = dot(left, right, 1, 0)
                total = term if total is None else total + term
            for hop in range(groups):
                piece = total[hop * part : (hop + 1) * part]
                outs[hop][expert] = piece.astype(outs[hop].dtype)

    results = call(
        kernel,
        [struct((experts, part, wide), BF16 if hop else F32) for hop in range(groups)],
        (weighted, *[array for array, _ in blocks]),
        [VMEM] * (1 + size),
        wait,
        cost=2 * experts * deep * size * rows * wide,
    )
    return results[0], results[1:]


def add_partials(owns, others, sets, wait=()):
    experts, part, wide = owns[0].shape
    chunks = len(owns)
    flat = [ref for chunk in range(chunks) for ref in (owns[chunk], *others[chunk])]
    each = len(flat) // chunks

    def kernel(*refs):
        outs = refs[len(flat) :]
        for chunk in range(chunks):
            for out, hops in zip(outs, sets):
                for at, hop in enumerate(hops):
                    total = refs[chunk * each][hop]
                    for ref in refs[chunk * each + 1 : (chunk + 1) * each]:
                        total = total + ref[hop].astype(F32)
                    out[at, chunk] = total.astype(out.dtype)

    return call(
        kernel,
        [struct((len(hops), chunks, part, wide), BF16 if hops[0] else F32) for hops in sets],
        flat,
        [VMEM] * len(flat),
        wait,
    )


def place_weight_grad(pieces, width, first, heads, before=None, wait=()):
    experts = len(pieces)
    _, many, part, _ = pieces[0].shape
    extra = [] if before is None else [before]
    slots = many * experts * 2

    def kernel(*refs):
        out_ref, token_ref, ready, sems = refs[experts + len(extra) :]
        token_ref[...] = jnp.zeros_like(token_ref)
        copies = []
        for number in range(many):
            for hop in range(experts):
                start = ((lax.axis_index("exp") ^ hop) * heads + first + number) * DH
                for side in range(2):
                    slot = (number * experts + hop) * 2 + side
                    ready[slot] = refs[hop][0, number, :, side * DH : (side + 1) * DH].astype(F32)
                    columns = pl.ds(pl.multiple_of(start + side * (width // 2), DH), DH)
                    copy = pltpu.make_async_copy(ready.at[slot], out_ref.at[0, :, columns], sems.at[slot])
                    copy.start()
                    copies.append(copy)
        for copy in copies:
            copy.wait()

    return call(
        kernel,
        [struct((1, part, width), F32), TOKEN],
        (*pieces, *extra),
        [VMEM] * experts + [HBM] * len(extra),
        wait,
        out_specs=[HBM, VMEM],
        scratch_shapes=[pltpu.VMEM((slots, part, DH), F32), pltpu.SemaphoreType.DMA((slots,))],
        input_output_aliases={experts: 0} if extra else {},
    )


def place_keys_values(packs, wait=()):
    where = [(pack, at) for pack in range(len(packs)) for at in range(packs[pack].shape[0])]
    heads = len(where)
    rows = packs[0].shape[1]

    def kernel(*refs):
        outs, token_ref, sems = refs[len(packs) : len(packs) + 2], refs[len(packs) + 2], refs[len(packs) + 3]
        token_ref[...] = jnp.zeros_like(token_ref)
        copies = []
        for number, (pack, at) in enumerate(where):
            for side in range(2):
                source = refs[pack].at[at, :, side * DH : (side + 1) * DH]
                target = outs[side].at[:, number * DH : (number + 1) * DH]
                copies.append(pltpu.make_async_copy(source, target, sems.at[number * 2 + side]))
        for copy in copies:
            copy.start()
        for copy in copies:
            copy.wait()

    return call(
        kernel,
        [struct((rows, heads * DH), BF16)] * 2 + [TOKEN],
        packs,
        [VMEM] * len(packs),
        wait,
        out_specs=[HBM] * 2 + [VMEM],
        scratch_shapes=[pltpu.SemaphoreType.DMA((2 * heads,))],
    )


def input_products(pieces, expert_weight, gate, wait=()):
    experts = len(pieces)
    packs = len(pieces[0])
    where = [(pack, at) for pack in range(packs) for at in range(pieces[0][pack].shape[0])]
    heads = len(where)
    rows = pieces[0][0].shape[1]
    _, wide, width = expert_weight.shape
    part = wide // experts
    even = experts // 2

    def kernel(w_ref, gate_ref, *refs):
        keep_ref, *send_refs = refs[experts * packs :]
        for out in range(experts):
            taken = pl.ds(pl.multiple_of((lax.axis_index("exp") ^ out) * part, part), part)
            total = None
            for hop in range(experts):
                for number, (pack, at) in enumerate(where):
                    start = ((lax.axis_index("exp") ^ hop) * heads + number) * DH
                    sides = [
                        w_ref[0, taken, pl.ds(pl.multiple_of(start + side * (width // 2), DH), DH)]
                        for side in range(2)
                    ]
                    term = dot(refs[hop * packs + pack][at], jnp.concatenate(sides, axis=1), 1, 1)
                    total = term if total is None else total + term
            total = gate_ref[...] * total
            if out % 2:
                send_refs[out // 2][...] = total.astype(BF16)
            else:
                keep_ref[out // 2] = total

    flat = [piece for row in pieces for piece in row]
    return call(
        kernel,
        [struct((even, rows, part), F32)] + [struct((rows, part), BF16)] * even,
        (expert_weight, gate, *flat),
        [VMEM] * (2 + len(flat)),
        wait,
        cost=2 * rows * wide * width,
    )


def add_parts(keep, arrived, wait=()):
    count, rows, wide = keep.shape
    half = count // 2

    def kernel(keep_ref, *refs):
        arrived_refs, outs = refs[:count], refs[count:]
        if not half:
            outs[1][...] = jnp.zeros_like(outs[1])
        for at in range(count):
            total = keep_ref[at] + arrived_refs[at][...].astype(F32)
            if at < half:
                outs[0][at] = total
            else:
                outs[at - half + min(half, 1)][...] = total.astype(BF16)

    if half:
        shapes = [struct((half, rows, wide), F32)] + [struct((rows, wide), BF16)] * (count - half)
    else:
        shapes = [struct((rows, wide), BF16), TOKEN]
    return call(kernel, shapes, (keep, *arrived), [VMEM] * (1 + count), wait)


def per_device(query, key, value, grad, inputs, expert_ids, route_gates, expert_weight):
    width = query.shape[1]
    heads = width // DH
    experts = lax.axis_size("exp")
    count = lax.axis_size("seq")
    size = 4
    groups = count // size
    many = heads // 2

    sent, own_columns, one, two, three, gate = begin(
        query, grad, inputs, expert_ids.T, route_gates.T, size, experts, count
    )
    by_two, relay = swap(two, "seq", 2), swap(three, "seq", 2)
    later = [swap(sent, "seq", 1)]
    other_state = own_states(key, value)
    total, sent = add_arrived(sent, later[0], [other_state])
    later.append(swap(sent, "seq", 2))
    mask = 4
    while 2 * mask < count:
        total, sent = add_arrived(total, later[-1])
        later.append(swap(sent, "seq", mask))
        mask *= 2
    sent = last_states(total, later[-1], other_state, [relay])
    came = swap(sent, "seq", mask)
    later.append(came)
    intra = [intra_keys_values(query, key, value, grad, 0, many, [sent])]
    intra.append(intra_keys_values(query, key, value, grad, many, heads - many, [intra[0]]))
    halves_of = [swap(one, "seq", 1), by_two, swap(relay, "seq", 1)]
    arrived = touch(halves_of)
    halves_of = [[half, swap(half, "exp", 1)] for half in halves_of]

    (lead,) = finish_keys_values(intra, key, value, later, [(0, None)], (), [intra[1], arrived])
    near = [(swap(lead, "seq", 1), None)]
    across = [(swap(lead, "seq", 2), None)]
    every, second, rest = finish_keys_values(
        intra, key, value, later, [(0, heads), (1, None), (2, heads - 2)], (lead,), [pair[1] for pair in halves_of]
    )
    packs = [every]
    weighted = weigh_inputs(own_columns, halves_of, experts)
    own_heads = [(every, at) for at in range(heads)]
    across.append((swap(second, "seq", 2), None))
    rest_across = swap(rest, "seq", 2)
    across += [(rest_across, at) for at in range(heads - 2)]
    far = [swap(pack, "exp", 2) for pack in packs]
    close = [swap(pack, "exp", 1) for pack in packs]
    pieces = [packs, close, far, [swap(pack, "exp", 1) for pack in far]]
    relayed = [(swap(after(across[0][0], near[0][0], weighted), "seq", 1), None)]
    owns, others = [], []
    close_token = touch(close)
    fillers = []
    for number in range(heads):
        if number:
            waits = [owns[number - 1]]
            if number >= 2:
                waits.append(touch(others[number - 2] + [owns[number - 1], close_token]))
            (mine, at), (passed, passed_at) = own_heads[number], across[number]
            stacked = stack(mine, passed, (at, passed_at), waits)
            pair = swap(stacked, "seq", 1)
            near.append((pair, 0))
            relayed.append((pair, 1))
        if number == 0:
            gradient_of_keys, value_grad, token = place_keys_values(packs, [weighted])
            fillers = [token]
        elif number == 1:
            intra_query = intra_queries(key, value, grad, [owns[0]])
            fillers = [intra_query]
        elif number == 2:
            fillers = []
        elif number == 3:
            total, sent = add_both(other_state, came, [owns[2], others[1][0]])
            earlier = [swap(sent, "seq", 1)]
            keep, *send = input_products(pieces, expert_weight, gate, [owns[2]])
            fillers = [touch(others[2])]
        own, other = weight_product(
            weighted, [own_heads[number], near[number], across[number], relayed[number]], groups, fillers
        )
        owns.append(own)
        others.append([shift(array, "seq", size * (hop + 1)) for hop, array in enumerate(other)])
    mask = 1
    while keep.ndim == 3:
        keep, *send = add_parts(keep, [swap(part, "exp", mask) for part in send])
        mask *= 2
    input_grad, input_token = keep, send[0]
    mask = 2
    while 2 * mask < count:
        total, sent = add_arrived(total, earlier[-1])
        earlier.append(swap(sent, "seq", mask))
        mask *= 2
    gradient_of_queries = finish_queries(intra_query, grad, came, earlier)

    hops = [[hop] for hop in range(experts)]
    weight_grad = None
    waits, placing = [], []
    for first, last in ((0, heads - 1), (heads - 1, heads)):
        own, *parts = add_partials(owns[first:last], others[first:last], hops, waits)
        parts = [own] + [swap(part, "exp", hop + 1) for hop, part in enumerate(parts)]
        weight_grad, token = place_weight_grad(
            parts, expert_weight.shape[2], first, heads, weight_grad, placing
        )
        waits, placing = [token], [input_token]
    return gradient_of_queries, gradient_of_keys, value_grad, input_grad, weight_grad


def solution(mesh):
    return jax.shard_map(
        per_device,
        mesh=mesh,
        in_specs=(
            P("seq", "exp"),
            P("seq", "exp"),
            P("seq", "exp"),
            P("seq", "exp"),
            P("seq", None),
            P("seq", None),
            P("seq", None),
            P("exp", None, None),
        ),
        out_specs=(
            P("seq", "exp"),
            P("seq", "exp"),
            P("seq", "exp"),
            P("seq", "exp"),
            P("exp", "seq", None),
        ),
        check_vma=False,
    )
```

```python
import functools

import jax
import jax.numpy as jnp
from jax import lax
from jax.experimental import pallas as pl
from jax.experimental.pallas import tpu as pltpu
from jax.sharding import PartitionSpec as P

DH = 128
PAD = 16
FIRST = 60.25
MIB = 1 << 20
BF16 = jnp.bfloat16
F32 = jnp.float32
VMEM = pl.BlockSpec(memory_space=pltpu.VMEM)
SMEM = pl.BlockSpec(memory_space=pltpu.SMEM)
HBM = pl.BlockSpec(memory_space=pltpu.HBM)


def struct(shape, dtype):
    return jax.ShapeDtypeStruct(shape, dtype)


TOKEN = struct((8, 128), F32)


def call(kernel, out_shape, operands, specs, wait=(), limit=16, cost=0, **options):
    known = len(operands)

    def body(*refs):
        kernel(*refs[:known], *refs[known + len(wait) :])

    grid = options.pop("grid", ())
    out_specs = options.pop("out_specs", VMEM)
    scratch = options.pop("scratch_shapes", ())
    prefetch = options.pop("prefetch", 0)
    if out_specs is VMEM and isinstance(out_shape, (list, tuple)):
        out_specs = [VMEM] * len(out_shape)
    return pl.pallas_call(
        body,
        out_shape=out_shape,
        grid_spec=pltpu.PrefetchScalarGridSpec(
            num_scalar_prefetch=prefetch,
            grid=grid,
            in_specs=list(specs) + [pl.BlockSpec(memory_space=pl.ANY)] * len(wait),
            out_specs=out_specs,
            scratch_shapes=scratch,
        ),
        cost_estimate=pl.CostEstimate(flops=cost, bytes_accessed=0, transcendentals=0),
        compiler_params=pltpu.CompilerParams(vmem_limit_bytes=int(limit * MIB)),
        **options,
    )(*operands, *wait)


def swap(array, axis, mask):
    count = lax.axis_size(axis)
    return lax.ppermute(array, axis, [(place, place ^ mask) for place in range(count)])


def shift(array, axis, step):
    count = lax.axis_size(axis)
    return lax.ppermute(array, axis, [(place, (place + step) % count) for place in range(count)])


def dot(a, b, left, right):
    return lax.dot_general(a, b, (((left,), (right,)), ((), ())), preferred_element_type=F32)


def head(ref, number):
    return ref[:, number * DH : (number + 1) * DH]


def after(array, *earlier):
    return lax.optimization_barrier((array, *earlier))[0]


def add_arrived(total, arrived, wait=()):
    def kernel(total_ref, arrived_ref, wide_ref, narrow_ref):
        added = total_ref[...].astype(F32) + arrived_ref[...].astype(F32)
        wide_ref[...] = added
        narrow_ref[...] = added.astype(BF16)

    shapes = [struct(total.shape, F32), struct(total.shape, BF16)]
    return call(kernel, shapes, (total, arrived), [VMEM] * 2, wait)


def touch(wait):
    def kernel(out_ref):
        out_ref[...] = jnp.zeros_like(out_ref)

    return call(kernel, TOKEN, (), (), wait)


def stack(first, second, at, wait=()):
    def kernel(a_ref, b_ref, out_ref):
        for place, ref in enumerate((a_ref, b_ref)):
            out_ref[place] = ref[...] if at[place] is None else ref[at[place]]

    return call(kernel, struct((2, *first.shape[-2:]), first.dtype), (first, second), [VMEM] * 2, wait)


def last_states(total, arrived, own, wait=()):
    def kernel(total_ref, arrived_ref, own_ref, out_ref):
        half = lax.axis_size("seq") // 2
        added = total_ref[...].astype(F32) + arrived_ref[...].astype(F32)
        out_ref[...] = jnp.where(lax.axis_index("seq") >= half, added.astype(BF16), own_ref[...])

    return call(kernel, struct(own.shape, BF16), (total, arrived, own), [VMEM] * 3, wait)


def later_state(refs, number):
    state = None
    for step, ref in enumerate(refs):
        lower = ((lax.axis_index("seq") >> step) & 1) == 0
        term = jnp.where(lower, ref[number].astype(F32), 0.0)
        state = term if state is None else state + term
    return state


def earlier_state(came_ref, refs, number):
    state = None
    half = came_ref[number].astype(F32)
    for step, ref in enumerate(refs):
        upper = ((lax.axis_index("seq") >> step) & 1) == 1
        term = jnp.where(upper, ref[0, number].astype(F32), 0.0)
        state = term if state is None else state + term
        half = half + ref[1, number].astype(F32)
    return state + jnp.where(lax.axis_index("seq") >= lax.axis_size("seq") // 2, half, 0.0)


def add_both(first, second, wait=()):
    def kernel(*refs):
        for at in range(2):
            for out in refs[2:]:
                out[at] = refs[at][...].astype(out.dtype)

    shape = (2, *first.shape)
    return call(kernel, [struct(shape, F32), struct(shape, BF16)], (first, second), [VMEM] * 2, wait)


def triangle(size, lower):
    down = lax.broadcasted_iota(jnp.int32, (size, size), 0)
    across = lax.broadcasted_iota(jnp.int32, (size, size), 1)
    return down >= across if lower else down <= across


def intra_keys_values(query, key, value, grad, first, many, wait=()):
    rows = query.shape[0]
    tile = rows // 2

    def kernel(q_ref, k_ref, v_ref, g_ref, out_ref):
        keep = triangle(tile, False)
        for number in range(many):
            q, k, v, g = (head(ref, first + number) for ref in (q_ref, k_ref, v_ref, g_ref))
            for down in range(2):
                here = slice(down * tile, (down + 1) * tile)
                rest = slice(down * tile, rows)
                for left, right, other, place in ((v, g, q, 0), (k, q, g, DH)):
                    scores = dot(left[here], right[rest], 1, 1)
                    kept = jnp.where(keep, scores[:, :tile], 0.0).astype(BF16)
                    if down == 0:
                        kept = jnp.concatenate([kept, scores[:, tile:].astype(BF16)], axis=1)
                    out_ref[number, here, place : place + DH] = dot(kept, other[rest], 1, 0)

    return call(
        kernel,
        struct((many, rows, 2 * DH), F32),
        (query, key, value, grad),
        [VMEM] * 4,
        wait,
        cost=24 * rows * rows * many * DH,
    )


def halves(state):
    high = state.astype(BF16)
    return high, (state - high.astype(F32)).astype(BF16)


def finish_keys_values(intra, key, value, arrived, sets, known=(), wait=()):
    where = [(array, at) for array in range(len(intra)) for at in range(intra[array].shape[0])]
    rows, wide = intra[0].shape[1:]
    needed = sorted({start + at for start, many in sets for at in range(many or 1)})

    def kernel(k_ref, v_ref, *refs):
        states, refs = refs[: len(arrived)], refs[len(arrived) :]
        intra_refs, refs = refs[: len(intra)], refs[len(intra) :]
        known_refs, outs = refs[: len(known)], refs[len(known) :]
        for number in needed:
            if number < len(known):
                both = known_refs[number][...]
            else:
                high, low = halves(later_state(states, number))
                v, k = head(v_ref, number), head(k_ref, number)
                by_key = dot(v, high, 1, 1) + dot(v, low, 1, 1)
                by_value = dot(k, high, 1, 0) + dot(k, low, 1, 0)
                array, at = where[number]
                both = intra_refs[array][at] + jnp.concatenate([by_key, by_value], axis=1)
                both = both.astype(BF16)
            for out, (start, many) in zip(outs, sets):
                if many is None and number == start:
                    out[...] = both
                elif many is not None and start <= number < start + many:
                    out[number - start] = both

    shapes = [struct((rows, wide) if many is None else (many, rows, wide), BF16) for _, many in sets]
    operands = (key, value, *arrived, *intra, *known)
    return call(kernel, shapes, operands, [VMEM] * len(operands), wait)


def intra_queries(key, value, grad, wait=()):
    rows, width = key.shape
    heads = width // DH
    tile = rows // 2

    def kernel(k_ref, v_ref, g_ref, out_ref):
        keep = triangle(tile, True)
        for number in range(heads):
            k, v, grad_of = head(k_ref, number), head(v_ref, number), head(g_ref, number)
            for down in range(2):
                upto = (down + 1) * tile
                g = grad_of[down * tile : upto]
                scores = dot(g, v[:upto], 1, 1)
                last = jnp.where(keep, scores[:, down * tile :], 0.0).astype(BF16)
                if down:
                    last = jnp.concatenate([scores[:, :tile].astype(BF16), last], axis=1)
                out_ref[down * tile : upto, number * DH : (number + 1) * DH] = dot(last, k[:upto], 1, 0)

    return call(
        kernel,
        struct((rows, width), F32),
        (key, value, grad),
        [VMEM] * 3,
        wait,
        cost=24 * rows * rows * width,
    )


def finish_queries(intra, grad, came, arrived, wait=()):
    rows, width = grad.shape
    heads = width // DH

    def kernel(intra_ref, g_ref, came_ref, *refs):
        out_ref, done, sems = refs[len(arrived) :]
        copies = []
        for number in range(heads):
            high, low = halves(earlier_state(came_ref, refs[: len(arrived)], number))
            columns = slice(number * DH, (number + 1) * DH)
            g = g_ref[:, columns]
            done[number] = (intra_ref[:, columns] + dot(g, high, 1, 1) + dot(g, low, 1, 1)).astype(BF16)
            copies.append(pltpu.make_async_copy(done.at[number], out_ref.at[:, columns], sems.at[number]))
            copies[-1].start()
        for copy in copies:
            copy.wait()

    return call(
        kernel,
        struct((rows, width), BF16),
        (intra, grad, came, *arrived),
        [VMEM] * (3 + len(arrived)),
        wait,
        out_specs=HBM,
        scratch_shapes=[pltpu.VMEM((heads, rows, DH), BF16), pltpu.SemaphoreType.DMA((heads,))],
    )


def begin(query, grad, inputs, ids, gates, size, experts, count):
    rows, width = query.shape
    wide = inputs.shape[1]
    heads = width // DH
    groups = count // size
    deep = wide // count
    half = rows // 2
    tall = groups * deep + PAD

    def kernel(*refs):
        me, mine_at = lax.axis_index("seq"), lax.axis_index("exp")
        sources, refs = refs[:5], refs[5:]
        sent_ref, refs = refs[0], refs[1:]
        outs, column_ref, refs = refs[:size], refs[size], refs[size + 1 :]
        held, sems, turned = refs[:5], refs[5], refs[6]
        copies = [
            pltpu.make_async_copy(source, target, sems.at[at])
            for at, (source, target) in enumerate(zip(sources, held))
        ]
        for copy in copies:
            copy.start()
        q_ref, g_ref, x_ref, id_ref, gate_ref = held
        copies[0].wait()
        copies[1].wait()
        for number in range(heads):
            sent_ref[number] = dot(head(q_ref, number), head(g_ref, number), 0, 0).astype(BF16)
        for copy in copies[2:]:
            copy.wait()
        step = DH * 2
        for start in range(0, wide, step):
            turned[start : start + step, :] = x_ref[:, start : start + step].astype(F32).T.astype(BF16)
        which = lax.broadcasted_iota(jnp.int32, (experts, rows), 0)
        weight = jnp.zeros((experts, rows), F32)
        for slot in range(ids.shape[0]):
            weight += jnp.where(id_ref[slot : slot + 1, :] == which, gate_ref[slot : slot + 1, :], 0.0)
        mine = jnp.sum(jnp.where(which == mine_at, weight, 0.0), axis=0, keepdims=True)
        column_ref[...] = jnp.broadcast_to(mine, (8, rows)).T[:, :1]
        parts = []
        for _ in range(3):
            part = weight.astype(BF16).astype(F32)
            parts.append(part)
            weight = weight - part
        tail = PAD - 3 * experts
        if tail:
            parts.append(jnp.zeros((tail, rows), F32))
        packed = jnp.concatenate(parts, axis=0)
        odd = mine_at & 1
        group, low = me // size, me % size
        columns = pl.ds(pl.multiple_of(odd * half, half), half)
        side = jnp.where(odd == 1, packed[:, half:], packed[:, :half]).astype(BF16)
        for member in range(size):
            for hop in range(groups):
                block = lax.rem(group + hop, groups) * size + (low ^ member)
                source = pl.ds(pl.multiple_of(block * deep, deep), deep)
                part = turned[source, columns] if member else turned[source, :]
                outs[member][hop * deep : (hop + 1) * deep, :] = part
            outs[member][groups * deep :, :] = side if member else packed.astype(BF16)

    messages = [struct((tall, half if member else rows), BF16) for member in range(size)]
    return call(
        kernel,
        [struct((heads, DH, DH), BF16)] + messages + [struct((rows, 1), F32)],
        (query, grad, inputs, ids, gates),
        [HBM] * 5,
        limit=FIRST,
        cost=12 * rows * width * DH,
        scratch_shapes=[pltpu.VMEM((rows, width), BF16)] * 2
        + [
            pltpu.VMEM((rows, wide), BF16),
            pltpu.VMEM(ids.shape, jnp.int32),
            pltpu.VMEM(gates.shape, F32),
            pltpu.SemaphoreType.DMA((5,)),
            pltpu.VMEM((wide, rows), BF16),
        ],
    )


def own_states(first, second):
    rows, width = first.shape
    heads = width // DH

    def kernel(a_ref, b_ref, out_ref):
        for number in range(heads):
            out_ref[number] = dot(head(a_ref, number), head(b_ref, number), 0, 0).astype(BF16)

    shape = struct((heads, DH, DH), BF16)
    return call(kernel, shape, (first, second), [VMEM] * 2, cost=6 * rows * width * DH)


def weigh_inputs(own, halves_of, experts, wait=()):
    deep, rows = own.shape
    deep -= PAD
    half = rows // 2
    size = 1 + len(halves_of)
    flat = [entry for pair in halves_of for entry in pair]

    def kernel(own_ref, *refs):
        out_ref = refs[len(flat)]
        odd = lax.axis_index("exp") & 1
        for at in range(1 + len(flat)):
            ref = own_ref if at == 0 else refs[at - 1]
            columns = ref[:deep, :].astype(F32)
            parts = ref[deep:, :].astype(F32)
            row = lax.broadcasted_iota(jnp.int32, parts.shape, 0)
            for step in range(experts):
                mine = (row < 3 * experts) & (lax.rem(row, experts) == (step ^ lax.axis_index("exp")))
                weight = jnp.sum(jnp.where(mine, parts, 0.0), axis=0, keepdims=True)
                scaled = (columns * weight).astype(BF16)
                if at == 0:
                    out_ref[step, :, :rows] = scaled
                else:
                    side = odd if at % 2 else 1 - odd
                    start = pl.multiple_of((at + 1) // 2 * rows + side * half, half)
                    out_ref[step, :, pl.ds(start, half)] = scaled

    return call(
        kernel,
        struct((experts, deep, size * rows), BF16),
        (own, *flat),
        [VMEM] * (1 + len(flat)),
        wait,
    )


def weight_product(weighted, blocks, groups, wait=()):
    experts, deep, _ = weighted.shape
    rows, wide = blocks[0][0].shape[-2:]
    size = len(blocks)
    part = deep // groups

    def kernel(w_ref, *refs):
        outs = refs[size:]
        for expert in range(experts):
            total = None
            for member in range(size):
                left = w_ref[expert, :, member * rows : (member + 1) * rows]
                at = blocks[member][1]
                right = refs[member][...] if at is None else refs[member][at]
                term = dot(left, right, 1, 0)
                total = term if total is None else total + term
            for hop in range(groups):
                piece = total[hop * part : (hop + 1) * part]
                outs[hop][expert] = piece.astype(outs[hop].dtype)

    results = call(
        kernel,
        [struct((experts, part, wide), BF16 if hop else F32) for hop in range(groups)],
        (weighted, *[array for array, _ in blocks]),
        [VMEM] * (1 + size),
        wait,
        cost=2 * experts * deep * size * rows * wide,
    )
    return results[0], results[1:]


def add_partials(owns, others, sets, wait=()):
    experts, part, wide = owns[0].shape
    chunks = len(owns)
    flat = [ref for chunk in range(chunks) for ref in (owns[chunk], *others[chunk])]
    each = len(flat) // chunks

    def kernel(*refs):
        outs = refs[len(flat) :]
        for chunk in range(chunks):
            for out, hops in zip(outs, sets):
                for at, hop in enumerate(hops):
                    total = refs[chunk * each][hop]
                    for ref in refs[chunk * each + 1 : (chunk + 1) * each]:
                        total = total + ref[hop].astype(F32)
                    out[at, chunk] = total.astype(out.dtype)

    return call(
        kernel,
        [struct((len(hops), chunks, part, wide), BF16 if hops[0] else F32) for hops in sets],
        flat,
        [VMEM] * len(flat),
        wait,
    )


def place_weight_grad(pieces, width, first, heads, before=None, wait=()):
    experts = len(pieces)
    _, many, part, _ = pieces[0].shape
    extra = [] if before is None else [before]
    slots = many * experts * 2

    def kernel(*refs):
        out_ref, token_ref, ready, sems = refs[experts + len(extra) :]
        token_ref[...] = jnp.zeros_like(token_ref)
        copies = []
        for number in range(many):
            for hop in range(experts):
                start = ((lax.axis_index("exp") ^ hop) * heads + first + number) * DH
                for side in range(2):
                    slot = (number * experts + hop) * 2 + side
                    ready[slot] = refs[hop][0, number, :, side * DH : (side + 1) * DH].astype(F32)
                    columns = pl.ds(pl.multiple_of(start + side * (width // 2), DH), DH)
                    copy = pltpu.make_async_copy(ready.at[slot], out_ref.at[0, :, columns], sems.at[slot])
                    copy.start()
                    copies.append(copy)
        for copy in copies:
            copy.wait()

    return call(
        kernel,
        [struct((1, part, width), F32), TOKEN],
        (*pieces, *extra),
        [VMEM] * experts + [HBM] * len(extra),
        wait,
        out_specs=[HBM, VMEM],
        scratch_shapes=[pltpu.VMEM((slots, part, DH), F32), pltpu.SemaphoreType.DMA((slots,))],
        input_output_aliases={experts: 0} if extra else {},
    )


def place_keys_values(packs, wait=()):
    where = [(pack, at) for pack in range(len(packs)) for at in range(packs[pack].shape[0])]
    heads = len(where)
    rows = packs[0].shape[1]

    def kernel(*refs):
        outs, token_ref, sems = refs[len(packs) : len(packs) + 2], refs[len(packs) + 2], refs[len(packs) + 3]
        token_ref[...] = jnp.zeros_like(token_ref)
        copies = []
        for number, (pack, at) in enumerate(where):
            for side in range(2):
                source = refs[pack].at[at, :, side * DH : (side + 1) * DH]
                target = outs[side].at[:, number * DH : (number + 1) * DH]
                copies.append(pltpu.make_async_copy(source, target, sems.at[number * 2 + side]))
        for copy in copies:
            copy.start()
        for copy in copies:
            copy.wait()

    return call(
        kernel,
        [struct((rows, heads * DH), BF16)] * 2 + [TOKEN],
        packs,
        [VMEM] * len(packs),
        wait,
        out_specs=[HBM] * 2 + [VMEM],
        scratch_shapes=[pltpu.SemaphoreType.DMA((2 * heads,))],
    )


def input_products(pieces, expert_weight, gate, wait=()):
    experts = len(pieces)
    packs = len(pieces[0])
    where = [(pack, at) for pack in range(packs) for at in range(pieces[0][pack].shape[0])]
    heads = len(where)
    rows = pieces[0][0].shape[1]
    _, wide, width = expert_weight.shape
    part = wide // experts
    even = experts // 2

    def kernel(w_ref, gate_ref, *refs):
        keep_ref, *send_refs = refs[experts * packs :]
        for out in range(experts):
            taken = pl.ds(pl.multiple_of((lax.axis_index("exp") ^ out) * part, part), part)
            total = None
            for hop in range(experts):
                for number, (pack, at) in enumerate(where):
                    start = ((lax.axis_index("exp") ^ hop) * heads + number) * DH
                    sides = [
                        w_ref[0, taken, pl.ds(pl.multiple_of(start + side * (width // 2), DH), DH)]
                        for side in range(2)
                    ]
                    term = dot(refs[hop * packs + pack][at], jnp.concatenate(sides, axis=1), 1, 1)
                    total = term if total is None else total + term
            total = gate_ref[...] * total
            if out % 2:
                send_refs[out // 2][...] = total.astype(BF16)
            else:
                keep_ref[out // 2] = total

    flat = [piece for row in pieces for piece in row]
    return call(
        kernel,
        [struct((even, rows, part), F32)] + [struct((rows, part), BF16)] * even,
        (expert_weight, gate, *flat),
        [VMEM] * (2 + len(flat)),
        wait,
        cost=2 * rows * wide * width,
    )


def add_parts(keep, arrived, wait=()):
    count, rows, wide = keep.shape
    half = count // 2

    def kernel(keep_ref, *refs):
        arrived_refs, outs = refs[:count], refs[count:]
        if not half:
            outs[1][...] = jnp.zeros_like(outs[1])
        for at in range(count):
            total = keep_ref[at] + arrived_refs[at][...].astype(F32)
            if at < half:
                outs[0][at] = total
            else:
                outs[at - half + min(half, 1)][...] = total.astype(BF16)

    if half:
        shapes = [struct((half, rows, wide), F32)] + [struct((rows, wide), BF16)] * (count - half)
    else:
        shapes = [struct((rows, wide), BF16), TOKEN]
    return call(kernel, shapes, (keep, *arrived), [VMEM] * (1 + count), wait)


def per_device(query, key, value, grad, inputs, expert_ids, route_gates, expert_weight):
    width = query.shape[1]
    heads = width // DH
    experts = lax.axis_size("exp")
    count = lax.axis_size("seq")
    size = 4
    groups = count // size
    many = heads // 2

    sent, own_columns, one, two, three, gate = begin(
        query, grad, inputs, expert_ids.T, route_gates.T, size, experts, count
    )
    by_two, relay = swap(two, "seq", 2), swap(three, "seq", 2)
    later = [swap(sent, "seq", 1)]
    other_state = own_states(key, value)
    total, sent = add_arrived(sent, later[0], [other_state])
    later.append(swap(sent, "seq", 2))
    mask = 4
    while 2 * mask < count:
        total, sent = add_arrived(total, later[-1])
        later.append(swap(sent, "seq", mask))
        mask *= 2
    sent = last_states(total, later[-1], other_state, [relay])
    came = swap(sent, "seq", mask)
    later.append(came)
    intra = [intra_keys_values(query, key, value, grad, 0, many, [sent])]
    intra.append(intra_keys_values(query, key, value, grad, many, heads - many, [intra[0]]))
    halves_of = [swap(one, "seq", 1), by_two, swap(relay, "seq", 1)]
    arrived = touch(halves_of)
    halves_of = [[half, swap(half, "exp", 1)] for half in halves_of]

    (lead,) = finish_keys_values(intra, key, value, later, [(0, None)], (), [intra[1], arrived])
    near = [(swap(lead, "seq", 1), None)]
    across = [(swap(lead, "seq", 2), None)]
    every, second, rest = finish_keys_values(
        intra, key, value, later, [(0, heads), (1, None), (2, heads - 2)], (lead,), [pair[1] for pair in halves_of]
    )
    packs = [every]
    weighted = weigh_inputs(own_columns, halves_of, experts)
    own_heads = [(every, at) for at in range(heads)]
    across.append((swap(second, "seq", 2), None))
    rest_across = swap(rest, "seq", 2)
    across += [(rest_across, at) for at in range(heads - 2)]
    far = [swap(pack, "exp", 2) for pack in packs]
    close = [swap(pack, "exp", 1) for pack in packs]
    pieces = [packs, close, far, [swap(pack, "exp", 1) for pack in far]]
    relayed = [(swap(after(across[0][0], near[0][0], weighted), "seq", 1), None)]
    owns, others = [], []
    close_token = touch(close)
    fillers = []
    for number in range(heads):
        if number:
            waits = [owns[number - 1]]
            if number >= 2:
                waits.append(touch(others[number - 2] + [owns[number - 1], close_token]))
            (mine, at), (passed, passed_at) = own_heads[number], across[number]
            stacked = stack(mine, passed, (at, passed_at), waits)
            pair = swap(stacked, "seq", 1)
            near.append((pair, 0))
            relayed.append((pair, 1))
        if number == 0:
            gradient_of_keys, value_grad, token = place_keys_values(packs, [weighted])
            fillers = [token]
        elif number == 1:
            intra_query = intra_queries(key, value, grad, [owns[0]])
            fillers = [intra_query]
        elif number == 2:
            fillers = []
        elif number == 3:
            total, sent = add_both(other_state, came, [owns[2], others[1][0]])
            earlier = [swap(sent, "seq", 1)]
            keep, *send = input_products(pieces, expert_weight, gate, [owns[2]])
            fillers = []
        own, other = weight_product(
            weighted, [own_heads[number], near[number], across[number], relayed[number]], groups, fillers
        )
        owns.append(own)
        others.append([shift(array, "seq", size * (hop + 1)) for hop, array in enumerate(other)])
    mask = 1
    while keep.ndim == 3:
        keep, *send = add_parts(keep, [swap(part, "exp", mask) for part in send])
        mask *= 2
    input_grad, input_token = keep, send[0]
    mask = 2
    while 2 * mask < count:
        total, sent = add_arrived(total, earlier[-1])
        earlier.append(swap(sent, "seq", mask))
        mask *= 2
    gradient_of_queries = finish_queries(intra_query, grad, came, earlier)

    hops = [[hop] for hop in range(experts)]
    weight_grad = None
    waits, placing = [], []
    for first, last in ((0, heads - 1), (heads - 1, heads)):
        own, *parts = add_partials(owns[first:last], others[first:last], hops, waits)
        parts = [own] + [swap(part, "exp", hop + 1) for hop, part in enumerate(parts)]
        weight_grad, token = place_weight_grad(
            parts, expert_weight.shape[2], first, heads, weight_grad, placing
        )
        waits, placing = [token], [input_token]
    return gradient_of_queries, gradient_of_keys, value_grad, input_grad, weight_grad


def solution(mesh):
    return jax.shard_map(
        per_device,
        mesh=mesh,
        in_specs=(
            P("seq", "exp"),
            P("seq", "exp"),
            P("seq", "exp"),
            P("seq", "exp"),
            P("seq", None),
            P("seq", None),
            P("seq", None),
            P("exp", None, None),
        ),
        out_specs=(
            P("seq", "exp"),
            P("seq", "exp"),
            P("seq", "exp"),
            P("seq", "exp"),
            P("exp", "seq", None),
        ),
        check_vma=False,
    )
```
